32 devices in a mesh: row: 8 (over y, x, core), col: 4 (over z).
Axes of the slice: x: 2, y: 2, z: 4, core: 2. Of those that a mesh axis runs over, the one named last changes fastest.
Arguments:
- activations: bfloat16 [256, 32, 8192], P(('row', 'col')), may hold values from -6 to 6
- out_grads: bfloat16 [256, 32, 8192], P(('row', 'col')), may hold values from -6 to 6
- proj_in: bfloat16 [8192, 64], replicated, may hold values from -0.0625 to 0.0625
- proj_out: bfloat16 [8192, 64], replicated, may hold values from -0.0625 to 0.0625
- damp_level: int32 [4096], replicated, may hold values from 1 to 4
Outputs:
- factored: float32 [4096, 4096], P('row', 'col')
The draws below stay inside these ranges and needn't reach their ends.
All inputs are finite; a program needn't handle non-finite values.
Results may differ from the reference program's by a relative error of at most 0.0033.
Values may be sent and summed in bfloat16 or wider, within the bound.
No kernel may reach another device: no remote copies, remote signals or barrier semaphores. Data moves between devices by JAX's collectives and lax.ppermute only.
A program may use at most 64 MiB of HBM per device.

```python
import jax
import jax.numpy as jnp
from jax import lax

D = 8192
R = 64
PANEL = 128
TOK_EX = 32
K = 4096
EXAMPLES = 256


def place_ends(entries, key, smallest, top_value):
    longest = entries.shape.index(max(entries.shape))
    spots = []
    for shift in (0, 1):
        where = [jax.random.randint(jax.random.fold_in(key, axis), (), 0, length) for axis, length in enumerate(entries.shape)]
        where[longest] = (where[longest] + shift) % entries.shape[longest]
        spots.append(tuple(where))
    return entries.at[spots[0]].set(smallest).at[spots[1]].set(top_value)


def block_scale(key, shape, cuts, smallest, top_value):
    level = 1.0
    for axis_at, blocks in cuts:
        draws = jax.random.uniform(jax.random.fold_in(jax.random.fold_in(key, 6), axis_at), (blocks,), jnp.float32, smallest / len(cuts), top_value / len(cuts))
        level = level * jnp.repeat(jnp.exp(draws), shape[axis_at] // blocks).reshape((-1,) + (1,) * (len(shape) - 1 - axis_at))
    return level


def normal_values(rng, shape, deviation, limit, shards=(), kind=jnp.bfloat16):
    loudness = block_scale(rng, shape, shards, -0.22, 0.18) if shards else 1.0
    drawn = jax.random.normal(rng, shape, jnp.float32) * deviation * loudness
    return jnp.minimum(jnp.maximum(drawn, -limit), limit).astype(kind)


def setup_inputs(seed: int = 0) -> dict:
    splits = jax.random.split(jax.random.key(seed), 6)
    return {
        "activations": normal_values(splits[0], (EXAMPLES, TOK_EX, D), 1.0, 6.0, ((0, 32),)),
        "out_grads": normal_values(splits[1], (EXAMPLES, TOK_EX, D), 1.0, 6.0, ((0, 32),)),
        "proj_in": normal_values(splits[2], (D, R), D ** -0.5, 0.0625),
        "proj_out": normal_values(splits[3], (D, R), D ** -0.5, 0.0625),
        "damp_level": place_ends(jax.random.randint(splits[4], (K,), 1, 5), jax.random.fold_in(splits[4], 1), 1, 4).astype(jnp.int32),
    }


damp_coef = 0.25

def project_one(pair):
    act_one, grad_one, proj_a, proj_g = pair
    a_proj = jnp.dot(act_one.astype(jnp.float32), proj_a.astype(jnp.float32), precision=lax.Precision.HIGHEST)
    g_proj = jnp.dot(grad_one.astype(jnp.float32), proj_g.astype(jnp.float32), precision=lax.Precision.HIGHEST)
    outer = jnp.dot(g_proj.T, a_proj, precision=lax.Precision.HIGHEST) * TOK_EX ** (-0.5)
    return outer.reshape(-1).astype(jnp.bfloat16)

def reference(activations, out_grads, proj_in, proj_out, damp_level):
    grads = lax.map(lambda item: project_one((item[0], item[1], proj_in, proj_out)), (activations, out_grads))
    wide = grads.astype(jnp.float32)
    total_sq = jnp.sum(wide * wide)
    damping = damp_coef * total_sq / (EXAMPLES * K)
    fisher = jnp.dot(wide.T, wide, precision=lax.Precision.HIGHEST) / EXAMPLES
    diag_index = jnp.arange(K)
    fisher = fisher.at[diag_index, diag_index].add(damping * damp_level.astype(jnp.float32))
    for panel_no in range(2):
        first = panel_no * PANEL
        beyond = first + PANEL
        lower = jnp.linalg.cholesky(fisher[first:beyond, first:beyond])
        left_panel = jax.scipy.linalg.solve_triangular(lower, fisher[beyond:, first:beyond].T, lower=True).T
        update = jnp.dot(left_panel, left_panel.T, precision=lax.Precision.HIGHEST)
        fisher = fisher.at[beyond:, beyond:].add(-update)
        fisher = fisher.at[first:beyond, first:beyond].set(jnp.tril(lower))
        fisher = fisher.at[beyond:, first:beyond].set(left_panel)
        fisher = fisher.at[first:beyond, beyond:].set(jnp.zeros((PANEL, K - beyond), jnp.float32))
    return fisher
```

```python
import functools

import jax
import jax.numpy as jnp
from jax import lax
from jax.experimental import pallas as pl
from jax.experimental.pallas import tpu as pltpu
from jax.sharding import PartitionSpec as P

PANEL = 128
BOTH = 2 * PANEL
LANES = 128
SUB = 8
STRIP = 64

damp_coef = 0.25

HIGHEST = lax.Precision.HIGHEST
FIRSTS = (((0,), (0,)), ((), ()))
LASTS = (((1,), (1,)), ((), ()))
PLAIN = (((1,), (0,)), ((), ()))


def mxu(left, right, dims=PLAIN):
    return lax.dot_general(left, right, dims, preferred_element_type=jnp.float32)


def halves(value):
    high = value.astype(jnp.bfloat16)
    return high, (value - high.astype(jnp.float32)).astype(jnp.bfloat16)


def project_kernel(act_ref, out_ref, in_ref, proj_ref, packed_ref, a_acc, g_acc, *, local_ex, tok_len):
    step = pl.program_id(0)

    @pl.when(step == 0)
    def _():
        a_acc[...] = jnp.zeros_like(a_acc)
        g_acc[...] = jnp.zeros_like(g_acc)

    a_acc[...] += mxu(act_ref[...], in_ref[...])
    g_acc[...] += mxu(out_ref[...], proj_ref[...])

    @pl.when(step == pl.num_programs(0) - 1)
    def _():
        a_proj = a_acc[...]
        tokens, rank_dim = a_proj.shape
        pairs = rank_dim * rank_dim // LANES
        g_turned = g_acc[...].T
        example = lax.broadcasted_iota(jnp.int32, (local_ex, tokens), 0)
        owner = lax.broadcasted_iota(jnp.int32, (local_ex, tokens), 1) // tok_len
        own = jnp.where(example == owner, tok_len ** (-0.5), 0.0).astype(jnp.float32)
        per_pair = LANES // rank_dim
        parts = []
        for part in range(per_pair):
            spread = jnp.concatenate(
                [
                    g_turned[pair * per_pair + part : pair * per_pair + part + 1, :] * own
                    for pair in range(pairs)
                ],
                axis=0,
            )
            parts.append(jnp.dot(spread, a_proj, precision=HIGHEST))
        grads = jnp.concatenate(parts, axis=1).astype(jnp.bfloat16)
        wide = grads.astype(jnp.float32)
        square = jnp.sum(jnp.sum(wide * wide, axis=0, keepdims=True), axis=1, keepdims=True)
        rows = pairs * local_ex
        packed_ref[:rows, :] = grads
        row_at = lax.broadcasted_iota(jnp.int32, (local_ex, LANES), 0)
        lane_at = lax.broadcasted_iota(jnp.int32, (local_ex, LANES), 1)
        first = square.astype(jnp.bfloat16).astype(jnp.float32)
        second = (square - first).astype(jnp.bfloat16).astype(jnp.float32)
        third = square - first - second
        coded = jnp.where(
            lane_at == 0, first, jnp.where(lane_at == 1, second, jnp.where(lane_at == 2, third, 0.0))
        )
        packed_ref[rows:, :] = jnp.where(row_at == 0, coded, 0.0).astype(jnp.bfloat16)


def project(activations, out_grads, proj_in, proj_out):
    local_ex, tok_len, model_dim = activations.shape
    rank_dim = proj_in.shape[1]
    tokens = local_ex * tok_len
    pairs = rank_dim * rank_dim // LANES
    chunk = 1024
    packed = pl.pallas_call(
        functools.partial(project_kernel, local_ex=local_ex, tok_len=tok_len),
        grid=(model_dim // chunk,),
        in_specs=[
            pl.BlockSpec((tokens, chunk), lambda d: (0, d)),
            pl.BlockSpec((tokens, chunk), lambda d: (0, d)),
            pl.BlockSpec((chunk, rank_dim), lambda d: (d, 0)),
            pl.BlockSpec((chunk, rank_dim), lambda d: (d, 0)),
        ],
        out_specs=pl.BlockSpec(((pairs + 1) * local_ex, LANES), lambda d: (0, 0)),
        out_shape=jax.ShapeDtypeStruct(((pairs + 1) * local_ex, LANES), jnp.bfloat16),
        scratch_shapes=[
            pltpu.VMEM((tokens, rank_dim), jnp.float32),
            pltpu.VMEM((tokens, rank_dim), jnp.float32),
        ],
        compiler_params=pltpu.CompilerParams(vmem_limit_bytes=32 * 2**20),
        name="project",
    )(
        activations.reshape(tokens, model_dim),
        out_grads.reshape(tokens, model_dim),
        proj_in,
        proj_out,
    )
    return packed.reshape(pairs + 1, local_ex, LANES)


def eliminate(work_ref, done_ref):
    tiles = BOTH // LANES
    sub_at = lax.broadcasted_iota(jnp.int32, (SUB, LANES), 0)
    lane_at = lax.broadcasted_iota(jnp.int32, (SUB, LANES), 1)
    for start in range(0, BOTH, STRIP):
        here = start // LANES
        live = list(range(here, tiles)) + list(range(tiles, tiles + here + 1))
        groups = STRIP // SUB
        rows = [
            {t: work_ref[start + g * SUB : start + (g + 1) * SUB, t * LANES : (t + 1) * LANES] for t in live}
            for g in range(groups)
        ]
        pivots = [jnp.ones((SUB, LANES), jnp.float32) for _ in range(groups)]

        def column(index):
            lane = (start + index) % LANES
            return [
                jnp.broadcast_to(rows[g][here][:, lane : lane + 1], (SUB, LANES)) if g >= index // SUB else None
                for g in range(groups)
            ]

        now = column(0)
        for index in range(STRIP):
            g_now, s_now = divmod(index, SUB)
            pivot = now[g_now][s_now : s_now + 1, :]
            inverse = 1.0 / pivot
            pivots[g_now] = jnp.where(sub_at == s_now, pivot, pivots[g_now])
            later = None
            if index + 1 < STRIP:
                g_next, s_next = divmod(index + 1, SUB)
                raw = column(index + 1)
                factor = now[g_next][s_next : s_next + 1, :] * inverse
                later = [
                    raw[g] - now[g] * factor if g >= g_next else None for g in range(groups)
                ]
            scaled = {t: rows[g_now][t][s_now : s_now + 1, :] * inverse for t in live}
            for g in range(g_now, groups):
                weight = now[g]
                if g == g_now:
                    if s_now == SUB - 1:
                        continue
                    weight = jnp.where(sub_at > s_now, weight, 0.0)
                for t in live:
                    rows[g][t] = rows[g][t] - weight * scaled[t]
            now = later
        for g in range(groups):
            root = lax.rsqrt(pivots[g])
            for t in range(2 * tiles):
                at = slice(start + g * SUB, start + (g + 1) * SUB), slice(t * LANES, (t + 1) * LANES)
                if t not in live:
                    done_ref[at] = jnp.zeros((SUB, LANES), jnp.float32)
                    continue
                value = rows[g][t] * root
                if t == here:
                    value = jnp.where(lane_at + t * LANES >= sub_at + start + g * SUB, value, 0.0)
                done_ref[at] = value
        beyond = start + STRIP
        if beyond < BOTH:
            first = beyond // LANES * LANES
            last = BOTH + -(-beyond // LANES) * LANES
            right = done_ref[start:beyond, first:last]
            cuts = [beyond, beyond + STRIP] + ([BOTH] if beyond + STRIP < BOTH else [])
            for low, high in zip(cuts[:-1], cuts[1:]):
                left = done_ref[start:beyond, low:high]
                work_ref[low:high, first:last] -= lax.dot_general(
                    left, right, FIRSTS, precision=HIGHEST, preferred_element_type=jnp.float32
                )


def fisher_kernel(
    place_ref, level_ref, panel_level_ref, *refs, sources, row_blocks, col_blocks, total_ex, feats
):
    arrived = refs[:sources]
    out_ref = refs[sources]
    g_row, g_col, g_panel, work, done, lower, mix_high, mix_low, panel_mix, damp_ref = refs[sources + 1 :]
    step = pl.program_id(0)
    row_at, col_at = place_ref[0], place_ref[1]
    panel_blocks = BOTH // LANES
    here = arrived[0].shape[1]

    @pl.when(step == 0)
    def _():
        row_base = lax.rem(row_at, 2) * row_blocks
        col_base = 2 * row_blocks
        panel_base = col_base + col_blocks
        total = jnp.zeros((here, LANES), jnp.float32)
        for n, piece in enumerate(arrived):
            at = slice(n * here, (n + 1) * here)
            for b in range(panel_blocks):
                g_panel[at, b * LANES : (b + 1) * LANES] = piece[panel_base + b]
            for b in range(row_blocks):
                g_row[at, b * LANES : (b + 1) * LANES] = piece[row_base + b]
            for b in range(col_blocks):
                g_col[b // panel_blocks, at, b % panel_blocks * LANES : (b % panel_blocks + 1) * LANES] = piece[
                    col_base + b
                ]
            total += piece[panel_base + panel_blocks].astype(jnp.float32)
        total_sq = jnp.sum(jnp.sum(total, axis=0, keepdims=True), axis=1, keepdims=True)
        damping = damp_coef * total_sq / (total_ex * feats)
        damp_ref[...] = jnp.broadcast_to(damping, damp_ref.shape)
        panel = g_panel[...]
        rows_at = lax.broadcasted_iota(jnp.int32, (BOTH, BOTH), 0)
        cols_at = lax.broadcasted_iota(jnp.int32, (BOTH, BOTH), 1)
        same = rows_at == cols_at
        work[:, :BOTH] = mxu(panel, panel, FIRSTS) * (1.0 / total_ex) + jnp.where(
            same, damping * panel_level_ref[...], 0.0
        )
        work[:, BOTH:] = jnp.where(same, 1.0, 0.0)
        eliminate(work, done)
        lower[...] = done[:, :BOTH].T
        w_high, w_low = halves(done[:, BOTH:])
        mixed = mxu(panel, w_high, LASTS) + mxu(panel, w_low, LASTS)
        y_high, y_low = halves(mixed)
        cross = mxu(y_high, y_low, LASTS)
        outer = mxu(y_high, y_high, LASTS) + cross + cross.T
        ex_rows = lax.broadcasted_iota(jnp.int32, outer.shape, 0)
        ex_cols = lax.broadcasted_iota(jnp.int32, outer.shape, 1)
        mix = (jnp.where(ex_rows == ex_cols, 1.0, 0.0) - outer * (1.0 / total_ex)) * (1.0 / total_ex)
        mix_high[...], mix_low[...] = halves(mix)
        panel_mix[...] = mixed * (1.0 / total_ex)

    in_panel = (col_at == 0) & (step == 0)
    cols = g_col[step]
    weights = mxu(mix_high[...], cols) + mxu(mix_low[...], cols)
    weights = jnp.where(in_panel, panel_mix[...], weights)
    high, low = halves(weights)
    rows = g_row[...]
    tile = mxu(rows, high, FIRSTS) + mxu(rows, low, FIRSTS)
    row_span, width = tile.shape
    col_first = (col_at * pl.num_programs(0) + step) * width
    row_glob = row_at * row_span + lax.broadcasted_iota(jnp.int32, tile.shape, 0)
    col_glob = col_first + lax.broadcasted_iota(jnp.int32, tile.shape, 1)
    out_ref[...] = tile + jnp.where(row_glob == col_glob, damp_ref[0:1, 0:1] * level_ref[...], 0.0)

    @pl.when(row_at == 0)
    def _():
        out_ref[:BOTH, :] = jnp.where(in_panel, lower[...], 0.0)


def fisher(place, col_levels, panel_levels, arrived, row_blocks, col_blocks, total_ex, feats):
    row_span, col_span = row_blocks * LANES, col_blocks * LANES
    sources = len(arrived)
    examples = sources * arrived[0].shape[1]
    vmem = pl.BlockSpec(memory_space=pltpu.VMEM)
    return pl.pallas_call(
        functools.partial(
            fisher_kernel,
            sources=sources,
            row_blocks=row_blocks,
            col_blocks=col_blocks,
            total_ex=total_ex,
            feats=feats,
        ),
        grid=(col_span // BOTH,),
        in_specs=[
            pl.BlockSpec(memory_space=pltpu.SMEM),
            pl.BlockSpec((1, BOTH), lambda n: (0, n)),
            vmem,
        ]
        + [vmem] * sources,
        out_specs=pl.BlockSpec((row_span, BOTH), lambda n: (0, n)),
        out_shape=jax.ShapeDtypeStruct((row_span, col_span), jnp.float32),
        scratch_shapes=[
            pltpu.VMEM((examples, row_span), jnp.bfloat16),
            pltpu.VMEM((col_span // BOTH, examples, BOTH), jnp.bfloat16),
            pltpu.VMEM((examples, BOTH), jnp.bfloat16),
            pltpu.VMEM((BOTH, 2 * BOTH), jnp.float32),
            pltpu.VMEM((BOTH, 2 * BOTH), jnp.float32),
            pltpu.VMEM((BOTH, BOTH), jnp.float32),
            pltpu.VMEM((examples, examples), jnp.bfloat16),
            pltpu.VMEM((examples, examples), jnp.bfloat16),
            pltpu.VMEM((examples, BOTH), jnp.float32),
            pltpu.VMEM((SUB, LANES), jnp.float32),
        ],
        compiler_params=pltpu.CompilerParams(vmem_limit_bytes=48 * 2**20),
        name="fisher",
    )(place, col_levels, panel_levels, *arrived)


def swap(block, axis, mask):
    size = lax.axis_size(axis)
    return lax.ppermute(block, axis, [(n, n ^ mask) for n in range(size)])


def shards(activations, out_grads, proj_in, proj_out, damp_level):
    local_ex = activations.shape[0]
    feats = proj_in.shape[1] * proj_out.shape[1]
    n_rows = lax.axis_size("row")
    n_cols = lax.axis_size("col")
    total_ex = local_ex * n_rows * n_cols
    row_at = lax.axis_index("row")
    col_at = lax.axis_index("col")
    blocks = feats // LANES
    row_blocks = blocks // n_rows
    col_blocks = blocks // n_cols

    levels = damp_level.astype(jnp.float32).reshape(1, feats)
    col_levels = lax.dynamic_slice_in_dim(levels, col_at * col_blocks * LANES, col_blocks * LANES, axis=1)
    place = jnp.stack([row_at, col_at]).astype(jnp.int32)

    packed = project(activations, out_grads, proj_in, proj_out)
    along = [packed] + [swap(packed, "col", mask) for mask in range(n_cols - 1, 0, -1)]
    line = jnp.concatenate(along, axis=1)

    common = [
        lax.dynamic_slice_in_dim(line, col_at * col_blocks, col_blocks),
        line[: BOTH // LANES],
        line[blocks:],
    ]
    pair_at = row_at // 2

    def bundle(pair):
        wanted = lax.dynamic_slice_in_dim(line, pair * 2 * row_blocks, 2 * row_blocks)
        return jnp.concatenate([wanted] + common)

    own = bundle(pair_at)
    got = [own] + [swap(bundle(pair_at ^ mask), "row", 2 * mask) for mask in range(1, n_rows // 2)]
    arrived = got + [swap(piece, "row", 1) for piece in got]
    return fisher(
        place, col_levels, levels[:, :BOTH], arrived, row_blocks, col_blocks, total_ex, feats
    )


def solution(mesh):
    return jax.shard_map(
        shards,
        mesh=mesh,
        in_specs=(P(("row", "col"), None, None), P(("row", "col"), None, None), P(), P(), P()),
        out_specs=P("row", "col"),
        check_vma=False,
    )
```

```python
import functools

import jax
import jax.numpy as jnp
from jax import lax
from jax.experimental import pallas as pl
from jax.experimental.pallas import tpu as pltpu
from jax.sharding import PartitionSpec as P

PANEL = 128
BOTH = 2 * PANEL
LANES = 128
SUB = 8
STRIP = 64
AHEAD = 1

damp_coef = 0.25

HIGHEST = lax.Precision.HIGHEST
FIRSTS = (((0,), (0,)), ((), ()))
LASTS = (((1,), (1,)), ((), ()))
PLAIN = (((1,), (0,)), ((), ()))


def mxu(left, right, dims=PLAIN):
    return lax.dot_general(left, right, dims, preferred_element_type=jnp.float32)


def halves(value):
    high = value.astype(jnp.bfloat16)
    return high, (value - high.astype(jnp.float32)).astype(jnp.bfloat16)


import functools

import jax
import jax.numpy as jnp
from jax import lax
from jax.experimental import pallas as pl
from jax.experimental.pallas import tpu as pltpu
from jax.sharding import PartitionSpec as P

PANEL = 128
BOTH = 2 * PANEL
LANES = 128
SUB = 8
STRIP = 64

damp_coef = 0.25

HIGHEST = lax.Precision.HIGHEST
FIRSTS = (((0,), (0,)), ((), ()))
LASTS = (((1,), (1,)), ((), ()))
PLAIN = (((1,), (0,)), ((), ()))


def mxu(left, right, dims=PLAIN):
    return lax.dot_general(left, right, dims, preferred_element_type=jnp.float32)


def halves(value):
    high = value.astype(jnp.bfloat16)
    return high, (value - high.astype(jnp.float32)).astype(jnp.bfloat16)


def project_kernel(act_ref, out_ref, in_ref, proj_ref, packed_ref, a_acc, g_acc, *, local_ex, tok_len):
    step = pl.program_id(0)

    @pl.when(step == 0)
    def _():
        a_acc[...] = jnp.zeros_like(a_acc)
        g_acc[...] = jnp.zeros_like(g_acc)

    a_acc[...] += mxu(act_ref[...], in_ref[...])
    g_acc[...] += mxu(out_ref[...], proj_ref[...])

    @pl.when(step == pl.num_programs(0) - 1)
    def _():
        a_proj = a_acc[...]
        tokens, rank_dim = a_proj.shape
        pairs = rank_dim * rank_dim // LANES
        g_turned = g_acc[...].T
        example = lax.broadcasted_iota(jnp.int32, (local_ex, tokens), 0)
        owner = lax.broadcasted_iota(jnp.int32, (local_ex, tokens), 1) // tok_len
        own = jnp.where(example == owner, tok_len ** (-0.5), 0.0).astype(jnp.float32)
        per_pair = LANES // rank_dim
        parts = []
        for part in range(per_pair):
            spread = jnp.concatenate(
                [
                    g_turned[pair * per_pair + part : pair * per_pair + part + 1, :] * own
                    for pair in range(pairs)
                ],
                axis=0,
            )
            parts.append(jnp.dot(spread, a_proj, precision=HIGHEST))
        grads = jnp.concatenate(parts, axis=1).astype(jnp.bfloat16)
        wide = grads.astype(jnp.float32)
        square = jnp.sum(jnp.sum(wide * wide, axis=0, keepdims=True), axis=1, keepdims=True)
        rows = pairs * local_ex
        packed_ref[:rows, :] = grads
        row_at = lax.broadcasted_iota(jnp.int32, (local_ex, LANES), 0)
        lane_at = lax.broadcasted_iota(jnp.int32, (local_ex, LANES), 1)
        first = square.astype(jnp.bfloat16).astype(jnp.float32)
        second = (square - first).astype(jnp.bfloat16).astype(jnp.float32)
        third = square - first - second
        coded = jnp.where(
            lane_at == 0, first, jnp.where(lane_at == 1, second, jnp.where(lane_at == 2, third, 0.0))
        )
        packed_ref[rows:, :] = jnp.where(row_at == 0, coded, 0.0).astype(jnp.bfloat16)


def project(activations, out_grads, proj_in, proj_out):
    local_ex, tok_len, model_dim = activations.shape
    rank_dim = proj_in.shape[1]
    tokens = local_ex * tok_len
    pairs = rank_dim * rank_dim // LANES
    chunk = 1024
    packed = pl.pallas_call(
        functools.partial(project_kernel, local_ex=local_ex, tok_len=tok_len),
        grid=(model_dim // chunk,),
        in_specs=[
            pl.BlockSpec((tokens, chunk), lambda d: (0, d)),
            pl.BlockSpec((tokens, chunk), lambda d: (0, d)),
            pl.BlockSpec((chunk, rank_dim), lambda d: (d, 0)),
            pl.BlockSpec((chunk, rank_dim), lambda d: (d, 0)),
        ],
        out_specs=pl.BlockSpec(((pairs + 1) * local_ex, LANES), lambda d: (0, 0)),
        out_shape=jax.ShapeDtypeStruct(((pairs + 1) * local_ex, LANES), jnp.bfloat16),
        scratch_shapes=[
            pltpu.VMEM((tokens, rank_dim), jnp.float32),
            pltpu.VMEM((tokens, rank_dim), jnp.float32),
        ],
        compiler_params=pltpu.CompilerParams(vmem_limit_bytes=32 * 2**20),
        name="project",
    )(
        activations.reshape(tokens, model_dim),
        out_grads.reshape(tokens, model_dim),
        proj_in,
        proj_out,
    )
    return packed.reshape(pairs + 1, local_ex, LANES)


def eliminate(work_ref, done_ref):
    tiles = BOTH // LANES
    sub_at = lax.broadcasted_iota(jnp.int32, (SUB, LANES), 0)
    lane_at = lax.broadcasted_iota(jnp.int32, (SUB, LANES), 1)
    for start in range(0, BOTH, STRIP):
        here = start // LANES
        live = list(range(here, tiles)) + list(range(tiles, tiles + here + 1))
        groups = STRIP // SUB
        rows = [
            {t: work_ref[start + g * SUB : start + (g + 1) * SUB, t * LANES : (t + 1) * LANES] for t in live}
            for g in range(groups)
        ]
        pivots = [jnp.ones((SUB, LANES), jnp.float32) for _ in range(groups)]

        def column(index):
            lane = (start + index) % LANES
            return [
                jnp.broadcast_to(rows[g][here][:, lane : lane + 1], (SUB, LANES)) if g >= index // SUB else None
                for g in range(groups)
            ]

        now = column(0)
        for index in range(STRIP):
            g_now, s_now = divmod(index, SUB)
            pivot = now[g_now][s_now : s_now + 1, :]
            inverse = 1.0 / pivot
            pivots[g_now] = jnp.where(sub_at == s_now, pivot, pivots[g_now])
            later = None
            if index + 1 < STRIP:
                g_next, s_next = divmod(index + 1, SUB)
                raw = column(index + 1)
                factor = now[g_next][s_next : s_next + 1, :] * inverse
                later = [
                    raw[g] - now[g] * factor if g >= g_next else None for g in range(groups)
                ]
            scaled = {t: rows[g_now][t][s_now : s_now + 1, :] * inverse for t in live}
            for g in range(g_now, groups):
                weight = now[g]
                if g == g_now:
                    if s_now == SUB - 1:
                        continue
                    weight = jnp.where(sub_at > s_now, weight, 0.0)
                for t in live:
                    rows[g][t] = rows[g][t] - weight * scaled[t]
            now = later
        for g in range(groups):
            root = lax.rsqrt(pivots[g])
            for t in range(2 * tiles):
                at = slice(start + g * SUB, start + (g + 1) * SUB), slice(t * LANES, (t + 1) * LANES)
                if t not in live:
                    done_ref[at] = jnp.zeros((SUB, LANES), jnp.float32)
                    continue
                value = rows[g][t] * root
                if t == here:
                    value = jnp.where(lane_at + t * LANES >= sub_at + start + g * SUB, value, 0.0)
                done_ref[at] = value
        beyond = start + STRIP
        if beyond < BOTH:
            first = beyond // LANES * LANES
            last = BOTH + -(-beyond // LANES) * LANES
            right = done_ref[start:beyond, first:last]
            cuts = [beyond, beyond + STRIP] + ([BOTH] if beyond + STRIP < BOTH else [])
            for low, high in zip(cuts[:-1], cuts[1:]):
                left = done_ref[start:beyond, low:high]
                work_ref[low:high, first:last] -= lax.dot_general(
                    left, right, FIRSTS, precision=HIGHEST, preferred_element_type=jnp.float32
                )


def fisher_kernel(
    place_ref, level_ref, panel_level_ref, *refs, sources, row_blocks, col_blocks, total_ex, feats
):
    arrived = refs[:sources]
    out_ref = refs[sources]
    g_row, g_col, g_panel, work, done, lower, mix_high, mix_low, panel_mix, damp_ref = refs[sources + 1 :]
    step = pl.program_id(0)
    row_at, col_at = place_ref[0], place_ref[1]
    panel_blocks = BOTH // LANES
    here = arrived[0].shape[1]

    @pl.when(step == 0)
    def _():
        row_base = lax.rem(row_at, 2) * row_blocks
        col_base = 2 * row_blocks
        panel_base = col_base + col_blocks
        total = jnp.zeros((here, LANES), jnp.float32)
        for n, piece in enumerate(arrived):
            at = slice(n * here, (n + 1) * here)
            for b in range(panel_blocks):
                g_panel[at, b * LANES : (b + 1) * LANES] = piece[panel_base + b]
            for b in range(row_blocks):
                g_row[at, b * LANES : (b + 1) * LANES] = piece[row_base + b]
            for b in range(col_blocks):
                g_col[b // panel_blocks, at, b % panel_blocks * LANES : (b % panel_blocks + 1) * LANES] = piece[
                    col_base + b
                ]
            total += piece[panel_base + panel_blocks].astype(jnp.float32)
        total_sq = jnp.sum(jnp.sum(total, axis=0, keepdims=True), axis=1, keepdims=True)
        damping = damp_coef * total_sq / (total_ex * feats)
        damp_ref[...] = jnp.broadcast_to(damping, damp_ref.shape)
        panel = g_panel[...]
        rows_at = lax.broadcasted_iota(jnp.int32, (BOTH, BOTH), 0)
        cols_at = lax.broadcasted_iota(jnp.int32, (BOTH, BOTH), 1)
        same = rows_at == cols_at
        work[:, :BOTH] = mxu(panel, panel, FIRSTS) * (1.0 / total_ex) + jnp.where(
            same, damping * panel_level_ref[...], 0.0
        )
        work[:, BOTH:] = jnp.where(same, 1.0, 0.0)
        eliminate(work, done)
        lower[...] = done[:, :BOTH].T
        w_high, w_low = halves(done[:, BOTH:])
        mixed = mxu(panel, w_high, LASTS) + mxu(panel, w_low, LASTS)
        y_high, y_low = halves(mixed)
        cross = mxu(y_high, y_low, LASTS)
        outer = mxu(y_high, y_high, LASTS) + cross + cross.T
        ex_rows = lax.broadcasted_iota(jnp.int32, outer.shape, 0)
        ex_cols = lax.broadcasted_iota(jnp.int32, outer.shape, 1)
        mix = (jnp.where(ex_rows == ex_cols, 1.0, 0.0) - outer * (1.0 / total_ex)) * (1.0 / total_ex)
        mix_high[...], mix_low[...] = halves(mix)
        panel_mix[...] = mixed * (1.0 / total_ex)

    in_panel = (col_at == 0) & (step == 0)
    cols = g_col[step]
    weights = mxu(mix_high[...], cols) + mxu(mix_low[...], cols)
    weights = jnp.where(in_panel, panel_mix[...], weights)
    high, low = halves(weights)
    rows = g_row[...]
    tile = mxu(rows, high, FIRSTS) + mxu(rows, low, FIRSTS)
    row_span, width = tile.shape
    col_first = (col_at * pl.num_programs(0) + step) * width
    row_glob = row_at * row_span + lax.broadcasted_iota(jnp.int32, tile.shape, 0)
    col_glob = col_first + lax.broadcasted_iota(jnp.int32, tile.shape, 1)
    out_ref[...] = tile + jnp.where(row_glob == col_glob, damp_ref[0:1, 0:1] * level_ref[...], 0.0)

    @pl.when(row_at == 0)
    def _():
        out_ref[:BOTH, :] = jnp.where(in_panel, lower[...], 0.0)


def fisher(place, col_levels, panel_levels, arrived, row_blocks, col_blocks, total_ex, feats):
    row_span, col_span = row_blocks * LANES, col_blocks * LANES
    sources = len(arrived)
    examples = sources * arrived[0].shape[1]
    vmem = pl.BlockSpec(memory_space=pltpu.VMEM)
    return pl.pallas_call(
        functools.partial(
            fisher_kernel,
            sources=sources,
            row_blocks=row_blocks,
            col_blocks=col_blocks,
            total_ex=total_ex,
            feats=feats,
        ),
        grid=(col_span // BOTH,),
        in_specs=[
            pl.BlockSpec(memory_space=pltpu.SMEM),
            pl.BlockSpec((1, BOTH), lambda n: (0, n)),
            vmem,
        ]
        + [vmem] * sources,
        out_specs=pl.BlockSpec((row_span, BOTH), lambda n: (0, n)),
        out_shape=jax.ShapeDtypeStruct((row_span, col_span), jnp.float32),
        scratch_shapes=[
            pltpu.VMEM((examples, row_span), jnp.bfloat16),
            pltpu.VMEM((col_span // BOTH, examples, BOTH), jnp.bfloat16),
            pltpu.VMEM((examples, BOTH), jnp.bfloat16),
            pltpu.VMEM((BOTH, 2 * BOTH), jnp.float32),
            pltpu.VMEM((BOTH, 2 * BOTH), jnp.float32),
            pltpu.VMEM((BOTH, BOTH), jnp.float32),
            pltpu.VMEM((examples, examples), jnp.bfloat16),
            pltpu.VMEM((examples, examples), jnp.bfloat16),
            pltpu.VMEM((examples, BOTH), jnp.float32),
            pltpu.VMEM((SUB, LANES), jnp.float32),
        ],
        compiler_params=pltpu.CompilerParams(vmem_limit_bytes=48 * 2**20),
        name="fisher",
    )(place, col_levels, panel_levels, *arrived)


def swap(block, axis, mask):
    size = lax.axis_size(axis)
    return lax.ppermute(block, axis, [(n, n ^ mask) for n in range(size)])


def shards(activations, out_grads, proj_in, proj_out, damp_level):
    local_ex = activations.shape[0]
    feats = proj_in.shape[1] * proj_out.shape[1]
    n_rows = lax.axis_size("row")
    n_cols = lax.axis_size("col")
    total_ex = local_ex * n_rows * n_cols
    row_at = lax.axis_index("row")
    col_at = lax.axis_index("col")
    blocks = feats // LANES
    row_blocks = blocks // n_rows
    col_blocks = blocks // n_cols

    levels = damp_level.astype(jnp.float32).reshape(1, feats)
    col_levels = lax.dynamic_slice_in_dim(levels, col_at * col_blocks * LANES, col_blocks * LANES, axis=1)
    place = jnp.stack([row_at, col_at]).astype(jnp.int32)

    packed = project(activations, out_grads, proj_in, proj_out)
    along = [packed] + [swap(packed, "col", mask) for mask in range(n_cols - 1, 0, -1)]
    line = jnp.concatenate(along, axis=1)

    common = [
        lax.dynamic_slice_in_dim(line, col_at * col_blocks, col_blocks),
        line[: BOTH // LANES],
        line[blocks:],
    ]
    pair_at = row_at // 2

    def bundle(pair):
        wanted = lax.dynamic_slice_in_dim(line, pair * 2 * row_blocks, 2 * row_blocks)
        return jnp.concatenate([wanted] + common)

    own = bundle(pair_at)
    got = [own] + [swap(bundle(pair_at ^ mask), "row", 2 * mask) for mask in range(1, n_rows // 2)]
    arrived = got + [swap(piece, "row", 1) for piece in got]
    return fisher(
        place, col_levels, levels[:, :BOTH], arrived, row_blocks, col_blocks, total_ex, feats
    )


def solution(mesh):
    return jax.shard_map(
        shards,
        mesh=mesh,
        in_specs=(P(("row", "col"), None, None), P(("row", "col"), None, None), P(), P(), P()),
        out_specs=P("row", "col"),
        check_vma=False,
    )


def eliminate(work_ref, done_ref):
    tiles = BOTH // LANES
    groups = STRIP // SUB
    sub_at = lax.broadcasted_iota(jnp.int32, (SUB, LANES), 0)
    lane_at = lax.broadcasted_iota(jnp.int32, (SUB, LANES), 1)
    for start in range(0, BOTH, STRIP):
        here = start // LANES
        live = list(range(here, tiles)) + list(range(tiles, tiles + here + 1))
        rows = [
            {t: work_ref[start + g * SUB : start + (g + 1) * SUB, t * LANES : (t + 1) * LANES] for t in live}
            for g in range(groups)
        ]
        roots = []

        def spread(block, low, high):
            lane = start % LANES + block * SUB
            return [
                {
                    g: jnp.broadcast_to(rows[g][here][:, lane + m : lane + m + 1], (SUB, LANES))
                    for g in range(low, high)
                }
                for m in range(SUB)
            ]

        cols = spread(0, 0, groups)
        for block in range(groups):
            near = min(block + 1 + AHEAD, groups)
            ahead = spread(block + 1, block + 1, near) if block + 1 < groups else None
            pivots = jnp.ones((SUB, LANES), jnp.float32)
            inverses = []
            for j in range(SUB):
                lead = cols[j]
                pivot = lead[block][j : j + 1, :]
                inverse = 1.0 / pivot
                inverses.append(inverse)
                pivots = jnp.where(sub_at == j, pivot, pivots)
                for m in range(j + 1, SUB):
                    factor = lead[block][m : m + 1, :] * inverse
                    for g in cols[m]:
                        cols[m][g] = cols[m][g] - lead[g] * factor
                if ahead is not None:
                    for m in range(SUB):
                        factor = lead[block + 1][m : m + 1, :] * inverse
                        for g in ahead[m]:
                            ahead[m][g] = ahead[m][g] - lead[g] * factor
                scaled = {t: rows[block][t][j : j + 1, :] * inverse for t in live}
                for g in range(block, groups):
                    weight = lead[g]
                    if g == block:
                        if j == SUB - 1:
                            continue
                        weight = jnp.where(sub_at > j, weight, 0.0)
                    for t in live:
                        rows[g][t] = rows[g][t] - weight * scaled[t]
            roots.append(lax.rsqrt(pivots))
            if ahead is not None:
                cols = ahead
                for m, late in enumerate(spread(block + 1, near, groups)):
                    cols[m].update(late)
        for g in range(groups):
            for t in range(2 * tiles):
                at = slice(start + g * SUB, start + (g + 1) * SUB), slice(t * LANES, (t + 1) * LANES)
                if t not in live:
                    done_ref[at] = jnp.zeros((SUB, LANES), jnp.float32)
                    continue
                value = rows[g][t] * roots[g]
                if t == here:
                    value = jnp.where(lane_at + t * LANES >= sub_at + start + g * SUB, value, 0.0)
                done_ref[at] = value
        beyond = start + STRIP
        if beyond < BOTH:
            first = beyond // LANES * LANES
            last = BOTH + -(-beyond // LANES) * LANES
            right = done_ref[start:beyond, first:last]
            cuts = [beyond, beyond + STRIP] + ([BOTH] if beyond + STRIP < BOTH else [])
            for low, high in zip(cuts[:-1], cuts[1:]):
                left = done_ref[start:beyond, low:high]
                work_ref[low:high, first:last] -= lax.dot_general(
                    left, right, FIRSTS, precision=HIGHEST, preferred_element_type=jnp.float32
                )


def fisher_kernel(
    place_ref, level_ref, panel_level_ref, *refs, sources, row_blocks, col_blocks, total_ex, feats
):
    arrived = refs[:sources]
    out_ref = refs[sources]
    g_row, g_col, g_panel, work, done, lower, mix_high, mix_low, panel_mix, damp_ref = refs[sources + 1 :]
    step = pl.program_id(0)
    row_at, col_at = place_ref[0], place_ref[1]
    panel_blocks = BOTH // LANES
    here = arrived[0].shape[1]

    @pl.when(step == 0)
    def _():
        row_base = lax.rem(row_at, 2) * row_blocks
        col_base = 2 * row_blocks
        panel_base = col_base + col_blocks
        total = jnp.zeros((here, LANES), jnp.float32)
        for n, piece in enumerate(arrived):
            at = slice(n * here, (n + 1) * here)
            for b in range(panel_blocks):
                g_panel[at, b * LANES : (b + 1) * LANES] = piece[panel_base + b]
            for b in range(row_blocks):
                g_row[at, b * LANES : (b + 1) * LANES] = piece[row_base + b]
            for b in range(col_blocks):
                g_col[b // panel_blocks, at, b % panel_blocks * LANES : (b % panel_blocks + 1) * LANES] = piece[
                    col_base + b
                ]
            total += piece[panel_base + panel_blocks].astype(jnp.float32)
        total_sq = jnp.sum(jnp.sum(total, axis=0, keepdims=True), axis=1, keepdims=True)
        damping = damp_coef * total_sq / (total_ex * feats)
        damp_ref[...] = jnp.broadcast_to(damping, damp_ref.shape)
        panel = g_panel[...]
        rows_at = lax.broadcasted_iota(jnp.int32, (BOTH, BOTH), 0)
        cols_at = lax.broadcasted_iota(jnp.int32, (BOTH, BOTH), 1)
        same = rows_at == cols_at
        work[:, :BOTH] = mxu(panel, panel, FIRSTS) * (1.0 / total_ex) + jnp.where(
            same, damping * panel_level_ref[...], 0.0
        )
        work[:, BOTH:] = jnp.where(same, 1.0, 0.0)
        eliminate(work, done)
        lower[...] = done[:, :BOTH].T
        w_high, w_low = halves(done[:, BOTH:])
        mixed = mxu(panel, w_high, LASTS) + mxu(panel, w_low, LASTS)
        y_high, y_low = halves(mixed)
        cross = mxu(y_high, y_low, LASTS)
        outer = mxu(y_high, y_high, LASTS) + cross + cross.T
        ex_rows = lax.broadcasted_iota(jnp.int32, outer.shape, 0)
        ex_cols = lax.broadcasted_iota(jnp.int32, outer.shape, 1)
        mix = (jnp.where(ex_rows == ex_cols, 1.0, 0.0) - outer * (1.0 / total_ex)) * (1.0 / total_ex)
        mix_high[...], mix_low[...] = halves(mix)
        panel_mix[...] = mixed * (1.0 / total_ex)

    in_panel = (col_at == 0) & (step == 0)
    cols = g_col[step]
    weights = mxu(mix_high[...], cols) + mxu(mix_low[...], cols)
    weights = jnp.where(in_panel, panel_mix[...], weights)
    high, low = halves(weights)
    rows = g_row[...]
    tile = mxu(rows, high, FIRSTS) + mxu(rows, low, FIRSTS)
    row_span, width = tile.shape
    col_first = (col_at * pl.num_programs(0) + step) * width
    row_glob = row_at * row_span + lax.broadcasted_iota(jnp.int32, tile.shape, 0)
    col_glob = col_first + lax.broadcasted_iota(jnp.int32, tile.shape, 1)
    out_ref[...] = tile + jnp.where(row_glob == col_glob, damp_ref[0:1, 0:1] * level_ref[...], 0.0)

    @pl.when(row_at == 0)
    def _():
        out_ref[:BOTH, :] = jnp.where(in_panel, lower[...], 0.0)


def fisher(place, col_levels, panel_levels, arrived, row_blocks, col_blocks, total_ex, feats):
    row_span, col_span = row_blocks * LANES, col_blocks * LANES
    sources = len(arrived)
    examples = sources * arrived[0].shape[1]
    vmem = pl.BlockSpec(memory_space=pltpu.VMEM)
    return pl.pallas_call(
        functools.partial(
            fisher_kernel,
            sources=sources,
            row_blocks=row_blocks,
            col_blocks=col_blocks,
            total_ex=total_ex,
            feats=feats,
        ),
        grid=(col_span // BOTH,),
        in_specs=[
            pl.BlockSpec(memory_space=pltpu.SMEM),
            pl.BlockSpec((1, BOTH), lambda n: (0, n)),
            vmem,
        ]
        + [vmem] * sources,
        out_specs=pl.BlockSpec((row_span, BOTH), lambda n: (0, n)),
        out_shape=jax.ShapeDtypeStruct((row_span, col_span), jnp.float32),
        scratch_shapes=[
            pltpu.VMEM((examples, row_span), jnp.bfloat16),
            pltpu.VMEM((col_span // BOTH, examples, BOTH), jnp.bfloat16),
            pltpu.VMEM((examples, BOTH), jnp.bfloat16),
            pltpu.VMEM((BOTH, 2 * BOTH), jnp.float32),
            pltpu.VMEM((BOTH, 2 * BOTH), jnp.float32),
            pltpu.VMEM((BOTH, BOTH), jnp.float32),
            pltpu.VMEM((examples, examples), jnp.bfloat16),
            pltpu.VMEM((examples, examples), jnp.bfloat16),
            pltpu.VMEM((examples, BOTH), jnp.float32),
            pltpu.VMEM((SUB, LANES), jnp.float32),
        ],
        compiler_params=pltpu.CompilerParams(vmem_limit_bytes=48 * 2**20),
        name="fisher",
    )(place, col_levels, panel_levels, *arrived)


def swap(block, axis, mask):
    size = lax.axis_size(axis)
    return lax.ppermute(block, axis, [(n, n ^ mask) for n in range(size)])


def shards(activations, out_grads, proj_in, proj_out, damp_level):
    local_ex = activations.shape[0]
    feats = proj_in.shape[1] * proj_out.shape[1]
    n_rows = lax.axis_size("row")
    n_cols = lax.axis_size("col")
    total_ex = local_ex * n_rows * n_cols
    row_at = lax.axis_index("row")
    col_at = lax.axis_index("col")
    blocks = feats // LANES
    row_blocks = blocks // n_rows
    col_blocks = blocks // n_cols

    levels = damp_level.astype(jnp.float32).reshape(1, feats)
    col_levels = lax.dynamic_slice_in_dim(levels, col_at * col_blocks * LANES, col_blocks * LANES, axis=1)
    place = jnp.stack([row_at, col_at]).astype(jnp.int32)

    packed = project(activations, out_grads, proj_in, proj_out)
    along = [packed] + [swap(packed, "col", mask) for mask in range(n_cols - 1, 0, -1)]
    line = jnp.concatenate(along, axis=1)

    common = [
        lax.dynamic_slice_in_dim(line, col_at * col_blocks, col_blocks),
        line[: BOTH // LANES],
        line[blocks:],
    ]
    pair_at = row_at // 2

    def bundle(pair):
        wanted = lax.dynamic_slice_in_dim(line, pair * 2 * row_blocks, 2 * row_blocks)
        return jnp.concatenate([wanted] + common)

    own = bundle(pair_at)
    got = [own] + [swap(bundle(pair_at ^ mask), "row", 2 * mask) for mask in range(1, n_rows // 2)]
    arrived = got + [swap(piece, "row", 1) for piece in got]
    return fisher(
        place, col_levels, levels[:, :BOTH], arrived, row_blocks, col_blocks, total_ex, feats
    )


def solution(mesh):
    return jax.shard_map(
        shards,
        mesh=mesh,
        in_specs=(P(("row", "col"), None, None), P(("row", "col"), None, None), P(), P(), P()),
        out_specs=P("row", "col"),
        check_vma=False,
    )
```

```python
import functools

import jax
import jax.numpy as jnp
from jax import lax
from jax.experimental import pallas as pl
from jax.experimental.pallas import tpu as pltpu
from jax.sharding import PartitionSpec as P

PANEL = 128
BOTH = 2 * PANEL
LANES = 128
SUB = 8
STRIP = 64
AHEAD = 1

damp_coef = 0.25

HIGHEST = lax.Precision.HIGHEST
FIRSTS = (((0,), (0,)), ((), ()))
LASTS = (((1,), (1,)), ((), ()))
PLAIN = (((1,), (0,)), ((), ()))


def mxu(left, right, dims=PLAIN):
    return lax.dot_general(left, right, dims, preferred_element_type=jnp.float32)


def halves(value):
    high = value.astype(jnp.bfloat16)
    return high, (value - high.astype(jnp.float32)).astype(jnp.bfloat16)


def project_kernel(
    act_hbm, out_hbm, in_hbm, proj_hbm, packed_ref, act_buf, out_buf, in_buf, proj_buf, sems, *, local_ex, tok_len
):
    tokens, rank_dim = act_buf.shape[0], in_buf.shape[0]
    pieces = (in_hbm, in_buf), (act_hbm, act_buf), (proj_hbm, proj_buf), (out_hbm, out_buf)
    copies = [pltpu.make_async_copy(whole, buf, sems.at[n]) for n, (whole, buf) in enumerate(pieces)]
    for copy in copies:
        copy.start()
    for copy in copies:
        copy.wait()
    a_proj = mxu(act_buf[...], in_buf[...], LASTS)
    g_turned = mxu(out_buf[...], proj_buf[...], LASTS).T
    pairs = rank_dim * rank_dim // LANES
    example = lax.broadcasted_iota(jnp.int32, (local_ex, tokens), 0)
    owner = lax.broadcasted_iota(jnp.int32, (local_ex, tokens), 1) // tok_len
    own = jnp.where(example == owner, 1.0, 0.0).astype(jnp.float32)
    per_pair = LANES // rank_dim
    a_high, a_low = halves(a_proj)
    both = jnp.concatenate([a_high, a_low], axis=1)
    g_high, g_low = [half.astype(jnp.float32) for half in halves(g_turned * tok_len ** (-0.5))]

    def spread(source, part):
        picks = [source[n * per_pair + part : n * per_pair + part + 1, :] * own for n in range(pairs)]
        return jnp.concatenate(picks, axis=0).astype(jnp.bfloat16)

    parts = []
    for part in range(per_pair):
        wide = mxu(spread(g_high, part), both)
        parts.append(wide[:, :rank_dim] + wide[:, rank_dim:] + mxu(spread(g_low, part), a_high))
    grads = jnp.concatenate(parts, axis=1).astype(jnp.bfloat16)
    wide = grads.astype(jnp.float32)
    square = jnp.sum(wide * wide, axis=0, keepdims=True)
    rows = pairs * local_ex
    packed_ref[:rows, :] = grads
    row_at = lax.broadcasted_iota(jnp.int32, (local_ex, LANES), 0)
    first = square.astype(jnp.bfloat16).astype(jnp.float32)
    second = (square - first).astype(jnp.bfloat16).astype(jnp.float32)
    third = square - first - second
    coded = jnp.where(row_at == 0, first, jnp.where(row_at == 1, second, jnp.where(row_at == 2, third, 0.0)))
    packed_ref[rows:, :] = coded.astype(jnp.bfloat16)


def project(activations, out_grads, proj_in, proj_out):
    local_ex, tok_len, model_dim = activations.shape
    rank_dim = proj_in.shape[1]
    tokens = local_ex * tok_len
    pairs = rank_dim * rank_dim // LANES
    hbm = pl.BlockSpec(memory_space=pltpu.HBM)
    packed = pl.pallas_call(
        functools.partial(project_kernel, local_ex=local_ex, tok_len=tok_len),
        in_specs=[hbm] * 4,
        out_specs=pl.BlockSpec(memory_space=pltpu.VMEM),
        out_shape=jax.ShapeDtypeStruct(((pairs + 1) * local_ex, LANES), jnp.bfloat16),
        scratch_shapes=[
            pltpu.VMEM((tokens, model_dim), jnp.bfloat16),
            pltpu.VMEM((tokens, model_dim), jnp.bfloat16),
            pltpu.VMEM((rank_dim, model_dim), jnp.bfloat16),
            pltpu.VMEM((rank_dim, model_dim), jnp.bfloat16),
            pltpu.SemaphoreType.DMA((4,)),
        ],
        compiler_params=pltpu.CompilerParams(vmem_limit_bytes=32 * 2**20),
        name="project",
    )(
        activations.reshape(tokens, model_dim),
        out_grads.reshape(tokens, model_dim),
        proj_in.T,
        proj_out.T,
    )
    return packed.reshape(pairs + 1, local_ex, LANES)


def eliminate(work_ref, done_ref):
    tiles = BOTH // LANES
    groups = STRIP // SUB
    sub_at = lax.broadcasted_iota(jnp.int32, (SUB, LANES), 0)
    lane_at = lax.broadcasted_iota(jnp.int32, (SUB, LANES), 1)
    for start in range(0, BOTH, STRIP):
        here = start // LANES
        live = list(range(here, tiles)) + list(range(tiles, tiles + here + 1))
        rows = [
            {t: work_ref[start + g * SUB : start + (g + 1) * SUB, t * LANES : (t + 1) * LANES] for t in live}
            for g in range(groups)
        ]
        roots = []

        def spread(block, low, high):
            lane = start % LANES + block * SUB
            return [
                {
                    g: jnp.broadcast_to(rows[g][here][:, lane + m : lane + m + 1], (SUB, LANES))
                    for g in range(low, high)
                }
                for m in range(SUB)
            ]

        cols = spread(0, 0, groups)
        for block in range(groups):
            near = min(block + 1 + AHEAD, groups)
            ahead = spread(block + 1, block + 1, near) if block + 1 < groups else None
            pivots = jnp.ones((SUB, LANES), jnp.float32)
            inverses = []
            for j in range(SUB):
                lead = cols[j]
                pivot = lead[block][j : j + 1, :]
                inverse = 1.0 / pivot
                inverses.append(inverse)
                pivots = jnp.where(sub_at == j, pivot, pivots)
                for m in range(j + 1, SUB):
                    factor = lead[block][m : m + 1, :] * inverse
                    for g in cols[m]:
                        cols[m][g] = cols[m][g] - lead[g] * factor
                if ahead is not None:
                    for m in range(SUB):
                        factor = lead[block + 1][m : m + 1, :] * inverse
                        for g in ahead[m]:
                            ahead[m][g] = ahead[m][g] - lead[g] * factor
                scaled = {t: rows[block][t][j : j + 1, :] * inverse for t in live}
                for g in range(block, groups):
                    weight = lead[g]
                    if g == block:
                        if j == SUB - 1:
                            continue
                        weight = jnp.where(sub_at > j, weight, 0.0)
                    for t in live:
                        rows[g][t] = rows[g][t] - weight * scaled[t]
            roots.append(lax.rsqrt(pivots))
            if ahead is not None:
                cols = ahead
                for m, late in enumerate(spread(block + 1, near, groups)):
                    cols[m].update(late)
        for g in range(groups):
            for t in range(2 * tiles):
                at = slice(start + g * SUB, start + (g + 1) * SUB), slice(t * LANES, (t + 1) * LANES)
                if t not in live:
                    done_ref[at] = jnp.zeros((SUB, LANES), jnp.float32)
                    continue
                value = rows[g][t] * roots[g]
                if t == here:
                    value = jnp.where(lane_at + t * LANES >= sub_at + start + g * SUB, value, 0.0)
                done_ref[at] = value
        beyond = start + STRIP
        if beyond < BOTH:
            first = beyond // LANES * LANES
            last = BOTH + -(-beyond // LANES) * LANES
            right = done_ref[start:beyond, first:last]
            cuts = [beyond, beyond + STRIP] + ([BOTH] if beyond + STRIP < BOTH else [])
            for low, high in zip(cuts[:-1], cuts[1:]):
                left = done_ref[start:beyond, low:high]
                work_ref[low:high, first:last] -= lax.dot_general(
                    left, right, FIRSTS, precision=HIGHEST, preferred_element_type=jnp.float32
                )


def fisher_kernel(
    place_ref, level_ref, panel_level_ref, *refs, sources, row_blocks, col_blocks, total_ex, feats
):
    arrived = refs[:sources]
    out_ref = refs[sources]
    g_row, g_col, g_panel, work, done, lower, mix_high, mix_low, panel_mix, damp_ref = refs[sources + 1 :]
    step = pl.program_id(0)
    row_at, col_at = place_ref[0], place_ref[1]
    panel_blocks = BOTH // LANES
    here = arrived[0].shape[1]

    @pl.when(step == 0)
    def _():
        row_base = lax.rem(row_at, 2) * row_blocks
        col_base = 2 * row_blocks
        panel_base = col_base + col_blocks
        total = jnp.zeros((here, LANES), jnp.float32)
        for n, piece in enumerate(arrived):
            at = slice(n * here, (n + 1) * here)
            for b in range(panel_blocks):
                g_panel[at, b * LANES : (b + 1) * LANES] = piece[panel_base + b]
            for b in range(row_blocks):
                g_row[at, b * LANES : (b + 1) * LANES] = piece[row_base + b]
            for b in range(col_blocks):
                g_col[b // panel_blocks, at, b % panel_blocks * LANES : (b % panel_blocks + 1) * LANES] = piece[
                    col_base + b
                ]
            total += piece[panel_base + panel_blocks].astype(jnp.float32)
        total_sq = jnp.sum(jnp.sum(total, axis=0, keepdims=True), axis=1, keepdims=True)
        damping = damp_coef * total_sq / (total_ex * feats)
        damp_ref[...] = jnp.broadcast_to(damping, damp_ref.shape)
        panel = g_panel[...]
        rows_at = lax.broadcasted_iota(jnp.int32, (BOTH, BOTH), 0)
        cols_at = lax.broadcasted_iota(jnp.int32, (BOTH, BOTH), 1)
        same = rows_at == cols_at
        work[:, :BOTH] = mxu(panel, panel, FIRSTS) * (1.0 / total_ex) + jnp.where(
            same, damping * panel_level_ref[...], 0.0
        )
        work[:, BOTH:] = jnp.where(same, 1.0, 0.0)
        eliminate(work, done)
        lower[...] = done[:, :BOTH].T
        w_high, w_low = halves(done[:, BOTH:])
        mixed = mxu(panel, w_high, LASTS) + mxu(panel, w_low, LASTS)
        y_high, y_low = halves(mixed)
        cross = mxu(y_high, y_low, LASTS)
        outer = mxu(y_high, y_high, LASTS) + cross + cross.T
        ex_rows = lax.broadcasted_iota(jnp.int32, outer.shape, 0)
        ex_cols = lax.broadcasted_iota(jnp.int32, outer.shape, 1)
        mix = (jnp.where(ex_rows == ex_cols, 1.0, 0.0) - outer * (1.0 / total_ex)) * (1.0 / total_ex)
        mix_high[...], mix_low[...] = halves(mix)
        panel_mix[...] = mixed * (1.0 / total_ex)

    in_panel = (col_at == 0) & (step == 0)
    cols = g_col[step]
    weights = mxu(mix_high[...], cols) + mxu(mix_low[...], cols)
    weights = jnp.where(in_panel, panel_mix[...], weights)
    high, low = halves(weights)
    rows = g_row[...]
    tile = mxu(rows, high, FIRSTS) + mxu(rows, low, FIRSTS)
    row_span, width = tile.shape
    col_first = (col_at * pl.num_programs(0) + step) * width
    row_glob = row_at * row_span + lax.broadcasted_iota(jnp.int32, tile.shape, 0)
    col_glob = col_first + lax.broadcasted_iota(jnp.int32, tile.shape, 1)
    out_ref[...] = tile + jnp.where(row_glob == col_glob, damp_ref[0:1, 0:1] * level_ref[...], 0.0)

    @pl.when(row_at == 0)
    def _():
        out_ref[:BOTH, :] = jnp.where(in_panel, lower[...], 0.0)


def fisher(place, col_levels, panel_levels, arrived, row_blocks, col_blocks, total_ex, feats):
    row_span, col_span = row_blocks * LANES, col_blocks * LANES
    sources = len(arrived)
    examples = sources * arrived[0].shape[1]
    vmem = pl.BlockSpec(memory_space=pltpu.VMEM)
    return pl.pallas_call(
        functools.partial(
            fisher_kernel,
            sources=sources,
            row_blocks=row_blocks,
            col_blocks=col_blocks,
            total_ex=total_ex,
            feats=feats,
        ),
        grid=(col_span // BOTH,),
        in_specs=[
            pl.BlockSpec(memory_space=pltpu.SMEM),
            pl.BlockSpec((1, BOTH), lambda n: (0, n)),
            vmem,
        ]
        + [vmem] * sources,
        out_specs=pl.BlockSpec((row_span, BOTH), lambda n: (0, n)),
        out_shape=jax.ShapeDtypeStruct((row_span, col_span), jnp.float32),
        scratch_shapes=[
            pltpu.VMEM((examples, row_span), jnp.bfloat16),
            pltpu.VMEM((col_span // BOTH, examples, BOTH), jnp.bfloat16),
            pltpu.VMEM((examples, BOTH), jnp.bfloat16),
            pltpu.VMEM((BOTH, 2 * BOTH), jnp.float32),
            pltpu.VMEM((BOTH, 2 * BOTH), jnp.float32),
            pltpu.VMEM((BOTH, BOTH), jnp.float32),
            pltpu.VMEM((examples, examples), jnp.bfloat16),
            pltpu.VMEM((examples, examples), jnp.bfloat16),
            pltpu.VMEM((examples, BOTH), jnp.float32),
            pltpu.VMEM((SUB, LANES), jnp.float32),
        ],
        compiler_params=pltpu.CompilerParams(vmem_limit_bytes=48 * 2**20),
        name="fisher",
    )(place, col_levels, panel_levels, *arrived)


def swap(block, axis, mask):
    size = lax.axis_size(axis)
    return lax.ppermute(block, axis, [(n, n ^ mask) for n in range(size)])


def shards(activations, out_grads, proj_in, proj_out, damp_level):
    local_ex = activations.shape[0]
    feats = proj_in.shape[1] * proj_out.shape[1]
    n_rows = lax.axis_size("row")
    n_cols = lax.axis_size("col")
    total_ex = local_ex * n_rows * n_cols
    row_at = lax.axis_index("row")
    col_at = lax.axis_index("col")
    blocks = feats // LANES
    row_blocks = blocks // n_rows
    col_blocks = blocks // n_cols

    levels = damp_level.astype(jnp.float32).reshape(1, feats)
    col_levels = lax.dynamic_slice_in_dim(levels, col_at * col_blocks * LANES, col_blocks * LANES, axis=1)
    place = jnp.stack([row_at, col_at]).astype(jnp.int32)

    packed = project(activations, out_grads, proj_in, proj_out)
    along = [packed] + [swap(packed, "col", mask) for mask in range(n_cols - 1, 0, -1)]
    line = jnp.concatenate(along, axis=1)

    common = [
        lax.dynamic_slice_in_dim(line, col_at * col_blocks, col_blocks),
        line[: BOTH // LANES],
        line[blocks:],
    ]
    pair_at = row_at // 2

    def bundle(pair):
        wanted = lax.dynamic_slice_in_dim(line, pair * 2 * row_blocks, 2 * row_blocks)
        return jnp.concatenate([wanted] + common)

    own = bundle(pair_at)
    got = [own] + [swap(bundle(pair_at ^ mask), "row", 2 * mask) for mask in range(1, n_rows // 2)]
    arrived = got + [swap(piece, "row", 1) for piece in got]
    return fisher(
        place, col_levels, levels[:, :BOTH], arrived, row_blocks, col_blocks, total_ex, feats
    )


def solution(mesh):
    return jax.shard_map(
        shards,
        mesh=mesh,
        in_specs=(P(("row", "col"), None, None), P(("row", "col"), None, None), P(), P(), P()),
        out_specs=P("row", "col"),
        check_vma=False,
    )
```

```python
import functools
import itertools

import jax
import jax.numpy as jnp
from jax import lax
from jax.experimental import pallas as pl
from jax.experimental.pallas import tpu as pltpu
from jax.sharding import PartitionSpec as P

PANEL = 128
BOTH = 2 * PANEL
LANES = 128
SUB = 8
STRIP = 64
AHEAD = 1
FILL = 2

damp_coef = 0.25

HIGHEST = lax.Precision.HIGHEST
FIRSTS = (((0,), (0,)), ((), ()))
LASTS = (((1,), (1,)), ((), ()))
PLAIN = (((1,), (0,)), ((), ()))


def mxu(left, right, dims=PLAIN):
    return lax.dot_general(left, right, dims, preferred_element_type=jnp.float32)


def halves(value):
    high = value.astype(jnp.bfloat16)
    return high, (value - high.astype(jnp.float32)).astype(jnp.bfloat16)


CUTS = 8


def project_kernel(
    act_hbm, out_hbm, in_hbm, proj_hbm, packed_ref, act_buf, out_buf, in_buf, proj_buf, sems, *, local_ex, tok_len
):
    _, tokens, chunk = act_buf.shape
    rank_dim = in_buf.shape[1]
    pieces = (in_hbm, in_buf), (act_hbm, act_buf), (proj_hbm, proj_buf), (out_hbm, out_buf)
    copies = [
        [
            pltpu.make_async_copy(whole.at[:, pl.ds(n * chunk, chunk)], buf.at[n], sems.at[n, which])
            for which, (whole, buf) in enumerate(pieces)
        ]
        for n in range(CUTS)
    ]
    for group in copies:
        for copy in group:
            copy.start()
    a_proj = jnp.zeros((tokens, rank_dim), jnp.float32)
    g_proj = jnp.zeros((tokens, rank_dim), jnp.float32)
    for n, group in enumerate(copies):
        for copy in group:
            copy.wait()
        a_proj += mxu(act_buf[n], in_buf[n], LASTS)
        g_proj += mxu(out_buf[n], proj_buf[n], LASTS)
    g_turned = g_proj.T
    pairs = rank_dim * rank_dim // LANES
    example = lax.broadcasted_iota(jnp.int32, (local_ex, tokens), 0)
    owner = lax.broadcasted_iota(jnp.int32, (local_ex, tokens), 1) // tok_len
    own = jnp.where(example == owner, 1.0, 0.0).astype(jnp.float32)
    per_pair = LANES // rank_dim
    a_high, a_low = halves(a_proj)
    both = jnp.concatenate([a_high, a_low], axis=1)
    g_high, g_low = [half.astype(jnp.float32) for half in halves(g_turned * tok_len ** (-0.5))]

    def spread(source, part):
        picks = [source[n * per_pair + part : n * per_pair + part + 1, :] * own for n in range(pairs)]
        return jnp.concatenate(picks, axis=0).astype(jnp.bfloat16)

    parts = []
    for part in range(per_pair):
        wide = mxu(spread(g_high, part), both)
        parts.append(wide[:, :rank_dim] + wide[:, rank_dim:] + mxu(spread(g_low, part), a_high))
    grads = jnp.concatenate(parts, axis=1).astype(jnp.bfloat16)
    wide = grads.astype(jnp.float32)
    square = jnp.sum(wide * wide, axis=0, keepdims=True)
    rows = pairs * local_ex
    packed_ref[:rows, :] = grads
    row_at = lax.broadcasted_iota(jnp.int32, (local_ex, LANES), 0)
    first = square.astype(jnp.bfloat16).astype(jnp.float32)
    second = (square - first).astype(jnp.bfloat16).astype(jnp.float32)
    third = square - first - second
    coded = jnp.where(row_at == 0, first, jnp.where(row_at == 1, second, jnp.where(row_at == 2, third, 0.0)))
    packed_ref[rows:, :] = coded.astype(jnp.bfloat16)


def project(activations, out_grads, proj_in, proj_out):
    local_ex, tok_len, model_dim = activations.shape
    rank_dim = proj_in.shape[1]
    tokens = local_ex * tok_len
    pairs = rank_dim * rank_dim // LANES
    hbm = pl.BlockSpec(memory_space=pltpu.HBM)
    packed = pl.pallas_call(
        functools.partial(project_kernel, local_ex=local_ex, tok_len=tok_len),
        in_specs=[hbm] * 4,
        out_specs=pl.BlockSpec(memory_space=pltpu.VMEM),
        out_shape=jax.ShapeDtypeStruct(((pairs + 1) * local_ex, LANES), jnp.bfloat16),
        scratch_shapes=[
            pltpu.VMEM((CUTS, tokens, model_dim // CUTS), jnp.bfloat16),
            pltpu.VMEM((CUTS, tokens, model_dim // CUTS), jnp.bfloat16),
            pltpu.VMEM((CUTS, rank_dim, model_dim // CUTS), jnp.bfloat16),
            pltpu.VMEM((CUTS, rank_dim, model_dim // CUTS), jnp.bfloat16),
            pltpu.SemaphoreType.DMA((CUTS, 4)),
        ],
        compiler_params=pltpu.CompilerParams(vmem_limit_bytes=32 * 2**20),
        name="project",
    )(
        *[
            pltpu.with_memory_space_constraint(whole, pltpu.HBM)
            for whole in (
                activations.reshape(tokens, model_dim),
                out_grads.reshape(tokens, model_dim),
                proj_in.T,
                proj_out.T,
            )
        ]
    )
    return packed.reshape(pairs + 1, local_ex, LANES)


def eliminate(work_ref, done_ref, fillers):
    tiles = BOTH // LANES
    groups = STRIP // SUB
    sub_at = lax.broadcasted_iota(jnp.int32, (SUB, LANES), 0)
    lane_at = lax.broadcasted_iota(jnp.int32, (SUB, LANES), 1)
    for start in range(0, BOTH, STRIP):
        here = start // LANES
        live = list(range(here, tiles)) + list(range(tiles, tiles + here + 1))
        rows = [
            {t: work_ref[start + g * SUB : start + (g + 1) * SUB, t * LANES : (t + 1) * LANES] for t in live}
            for g in range(groups)
        ]
        roots = []

        def spread(block, low, high):
            lane = start % LANES + block * SUB
            return [
                {
                    g: jnp.broadcast_to(rows[g][here][:, lane + m : lane + m + 1], (SUB, LANES))
                    for g in range(low, high)
                }
                for m in range(SUB)
            ]

        cols = spread(0, 0, groups)
        for block in range(groups):
            near = min(block + 1 + AHEAD, groups)
            ahead = spread(block + 1, block + 1, near) if block + 1 < groups else None
            pivots = jnp.ones((SUB, LANES), jnp.float32)
            inverses = []
            for j in range(SUB):
                lead = cols[j]
                pivot = lead[block][j : j + 1, :]
                inverse = 1.0 / pivot
                inverses.append(inverse)
                pivots = jnp.where(sub_at == j, pivot, pivots)
                for m in range(j + 1, SUB):
                    factor = lead[block][m : m + 1, :] * inverse
                    for g in cols[m]:
                        cols[m][g] = cols[m][g] - lead[g] * factor
                if ahead is not None:
                    for m in range(SUB):
                        factor = lead[block + 1][m : m + 1, :] * inverse
                        for g in ahead[m]:
                            ahead[m][g] = ahead[m][g] - lead[g] * factor
                scaled = {t: rows[block][t][j : j + 1, :] * inverse for t in live}
                for g in range(block, groups):
                    weight = lead[g]
                    if g == block:
                        if j == SUB - 1:
                            continue
                        weight = jnp.where(sub_at > j, weight, 0.0)
                    for t in live:
                        rows[g][t] = rows[g][t] - weight * scaled[t]
            roots.append(lax.rsqrt(pivots))
            for filler in itertools.islice(fillers, FILL):
                filler()
            if ahead is not None:
                cols = ahead
                for m, late in enumerate(spread(block + 1, near, groups)):
                    cols[m].update(late)
        for g in range(groups):
            for t in range(2 * tiles):
                at = slice(start + g * SUB, start + (g + 1) * SUB), slice(t * LANES, (t + 1) * LANES)
                if t not in live:
                    done_ref[at] = jnp.zeros((SUB, LANES), jnp.float32)
                    continue
                value = rows[g][t] * roots[g]
                if t == here:
                    value = jnp.where(lane_at + t * LANES >= sub_at + start + g * SUB, value, 0.0)
                done_ref[at] = value
        beyond = start + STRIP
        if beyond < BOTH:
            first = beyond // LANES * LANES
            last = BOTH + -(-beyond // LANES) * LANES
            right = done_ref[start:beyond, first:last]
            cuts = [beyond, beyond + STRIP] + ([BOTH] if beyond + STRIP < BOTH else [])
            for low, high in zip(cuts[:-1], cuts[1:]):
                left = done_ref[start:beyond, low:high]
                work_ref[low:high, first:last] -= lax.dot_general(
                    left, right, FIRSTS, precision=HIGHEST, preferred_element_type=jnp.float32
                )


def fisher_kernel(
    place_ref, level_ref, panel_level_ref, *refs, sources, total_ex, feats
):
    arrived = refs[:sources]
    out_ref, g_panel, g_row, g_col, turned, work, done, weights, held, sems = refs[sources:]
    row_at, col_at = place_ref[0], place_ref[1]
    here = arrived[0].shape[1]
    row_span, col_span = held.shape
    row_blocks, col_blocks, panel_blocks = row_span // LANES, col_span // LANES, BOTH // LANES
    examples = sources * here
    col_base = 2 * row_blocks
    panel_base = col_base + col_blocks
    row_base = lax.rem(row_at, 2) * row_blocks

    def gather(target, base, blocks, n):
        for b in range(blocks):
            target[n * here : (n + 1) * here, b * LANES : (b + 1) * LANES] = arrived[n][base + b]

    total = jnp.zeros((here, LANES), jnp.float32)
    for n in range(sources):
        gather(g_panel, panel_base, panel_blocks, n)
        total += arrived[n][panel_base + panel_blocks].astype(jnp.float32)
    total_sq = jnp.sum(jnp.sum(total, axis=0, keepdims=True), axis=1, keepdims=True)
    damping = damp_coef * total_sq / (total_ex * feats)
    panel = g_panel[...]
    rows_at = lax.broadcasted_iota(jnp.int32, (BOTH, BOTH), 0)
    cols_at = lax.broadcasted_iota(jnp.int32, (BOTH, BOTH), 1)
    same = rows_at == cols_at
    work[:, :BOTH] = mxu(panel, panel, FIRSTS) * (1.0 / total_ex) + jnp.where(
        same, damping * panel_level_ref[...], 0.0
    )
    work[:, BOTH:] = jnp.where(same, 1.0, 0.0)

    def turn(first):
        turned[first : first + LANES, :] = g_row[:, first : first + LANES].T

    fillers = iter(
        [functools.partial(gather, g_row, row_base, row_blocks, n) for n in range(sources)]
        + [functools.partial(turn, first) for first in range(0, row_span, LANES)]
        + [functools.partial(gather, g_col, col_base, col_blocks, n) for n in range(sources)]
    )
    eliminate(work, done, fillers)
    for filler in fillers:
        filler()

    w_high, w_low = halves(done[:, BOTH:])
    mixed = mxu(panel, w_high, LASTS) + mxu(panel, w_low, LASTS)
    y_high, y_low = halves(mixed)
    cross = mxu(y_high, y_low, LASTS)
    outer = mxu(y_high, y_high, LASTS) + cross + cross.T
    ex_rows = lax.broadcasted_iota(jnp.int32, outer.shape, 0)
    ex_cols = lax.broadcasted_iota(jnp.int32, outer.shape, 1)
    mix = (jnp.where(ex_rows == ex_cols, 1.0, 0.0) - outer * (1.0 / total_ex)) * (1.0 / total_ex)
    both = jnp.concatenate(halves(mix), axis=1)
    for first in range(0, col_span, BOTH):
        lanes = slice(first, first + BOTH)
        cols = g_col[:, lanes]
        value = mxu(both, jnp.concatenate([cols, cols], axis=0))
        if first == 0:
            value = jnp.where(col_at == 0, mixed * (1.0 / total_ex), value)
        weights[:examples, lanes], weights[examples:, lanes] = halves(value)

    lower = done[:, :BOTH].T
    eye = lax.broadcasted_iota(jnp.int32, (LANES, LANES), 0) == lax.broadcasted_iota(
        jnp.int32, (LANES, LANES), 1
    )
    copies = []
    for strip in range(row_blocks):
        rows = slice(strip * LANES, (strip + 1) * LANES)
        left = turned[rows, :]
        held[rows, :] = mxu(jnp.concatenate([left, left], axis=1), weights[...])
        block = row_at * row_blocks + strip - col_at * col_blocks
        inside = (block >= 0) & (block < col_blocks)
        lanes = pl.ds(pl.multiple_of(jnp.clip(block, 0, col_blocks - 1) * LANES, LANES), LANES)
        held[rows, lanes] += jnp.where(eye & inside, level_ref[:, lanes] * damping, 0.0)
        if strip * LANES < BOTH:

            @pl.when(row_at == 0)
            def _(rows=rows):
                held[rows, :] = jnp.zeros((LANES, col_span), jnp.float32)
                held[rows, :BOTH] = jnp.where(col_at == 0, lower[rows, :], 0.0)

        copy = pltpu.make_async_copy(held.at[rows, :], out_ref.at[rows, :], sems.at[strip])
        copy.start()
        copies.append(copy)
    for copy in copies:
        copy.wait()


def fisher(place, col_levels, panel_levels, arrived, row_blocks, col_blocks, total_ex, feats):
    row_span, col_span = row_blocks * LANES, col_blocks * LANES
    sources = len(arrived)
    vmem = pl.BlockSpec(memory_space=pltpu.VMEM)
    return pl.pallas_call(
        functools.partial(fisher_kernel, sources=sources, total_ex=total_ex, feats=feats),
        in_specs=[pl.BlockSpec(memory_space=pltpu.SMEM)] + [vmem] * (2 + sources),
        out_specs=pl.BlockSpec(memory_space=pltpu.HBM),
        out_shape=jax.ShapeDtypeStruct((row_span, col_span), jnp.float32),
        scratch_shapes=[
            pltpu.VMEM((total_ex, BOTH), jnp.bfloat16),
            pltpu.VMEM((total_ex, row_span), jnp.bfloat16),
            pltpu.VMEM((total_ex, col_span), jnp.bfloat16),
            pltpu.VMEM((row_span, total_ex), jnp.bfloat16),
            pltpu.VMEM((BOTH, 2 * BOTH), jnp.float32),
            pltpu.VMEM((BOTH, 2 * BOTH), jnp.float32),
            pltpu.VMEM((2 * total_ex, col_span), jnp.bfloat16),
            pltpu.VMEM((row_span, col_span), jnp.float32),
            pltpu.SemaphoreType.DMA((row_blocks,)),
        ],
        compiler_params=pltpu.CompilerParams(vmem_limit_bytes=32 * 2**20),
        name="fisher",
    )(place, col_levels, panel_levels, *arrived)


def swap(block, axis, mask):
    size = lax.axis_size(axis)
    return lax.ppermute(block, axis, [(n, n ^ mask) for n in range(size)])


def shards(activations, out_grads, proj_in, proj_out, damp_level):
    local_ex = activations.shape[0]
    feats = proj_in.shape[1] * proj_out.shape[1]
    n_rows = lax.axis_size("row")
    n_cols = lax.axis_size("col")
    total_ex = local_ex * n_rows * n_cols
    row_at = lax.axis_index("row")
    col_at = lax.axis_index("col")
    blocks = feats // LANES
    row_blocks = blocks // n_rows
    col_blocks = blocks // n_cols

    levels = damp_level.astype(jnp.float32).reshape(1, feats)
    col_levels = lax.dynamic_slice_in_dim(levels, col_at * col_blocks * LANES, col_blocks * LANES, axis=1)
    place = jnp.stack([row_at, col_at]).astype(jnp.int32)

    packed = project(activations, out_grads, proj_in, proj_out)
    along = [packed] + [swap(packed, "col", mask) for mask in range(n_cols - 1, 0, -1)]
    line = jnp.concatenate(along, axis=1)

    common = [
        lax.dynamic_slice_in_dim(line, col_at * col_blocks, col_blocks),
        line[: BOTH // LANES],
        line[blocks:],
    ]
    pairs = n_rows // 2
    pair_at = row_at // 2

    def bundle(pair):
        wanted = lax.dynamic_slice_in_dim(line, pair * 2 * row_blocks, 2 * row_blocks)
        return jnp.concatenate([wanted] + common)

    got = [bundle(pair_at)] + [swap(bundle(pair_at ^ mask), "row", 2 * mask) for mask in range(1, pairs)]
    arrived = got + [swap(piece, "row", 1) for piece in got]
    return fisher(
        place, col_levels, levels[:, :BOTH], arrived, row_blocks, col_blocks, total_ex, feats
    )


def solution(mesh):
    return jax.shard_map(
        shards,
        mesh=mesh,
        in_specs=(P(("row", "col"), None, None), P(("row", "col"), None, None), P(), P(), P()),
        out_specs=P("row", "col"),
        check_vma=False,
    )
```

```python
import functools
import itertools

import jax
import jax.numpy as jnp
from jax import lax
from jax.experimental import pallas as pl
from jax.experimental.pallas import tpu as pltpu
from jax.sharding import PartitionSpec as P

PANEL = 128
BOTH = 2 * PANEL
LANES = 128
SUB = 8
STRIP = 64
AHEAD = 1
FILL = 2

damp_coef = 0.25

HIGHEST = lax.Precision.HIGHEST
FIRSTS = (((0,), (0,)), ((), ()))
LASTS = (((1,), (1,)), ((), ()))
PLAIN = (((1,), (0,)), ((), ()))


def mxu(left, right, dims=PLAIN):
    return lax.dot_general(left, right, dims, preferred_element_type=jnp.float32)


def halves(value):
    high = value.astype(jnp.bfloat16)
    return high, (value - high.astype(jnp.float32)).astype(jnp.bfloat16)


CUTS = 8


def thirds(value):
    high = value.astype(jnp.bfloat16)
    return (high, *halves(value - high.astype(jnp.float32)))


def project_kernel(
    act_hbm, out_hbm, in_hbm, proj_hbm, packed_ref, act_buf, out_buf, in_buf, proj_buf, sems, *, local_ex, tok_len
):
    _, tokens, chunk = act_buf.shape
    rank_dim = in_buf.shape[1]
    pieces = (in_hbm, in_buf), (act_hbm, act_buf), (proj_hbm, proj_buf), (out_hbm, out_buf)
    copies = [
        [
            pltpu.make_async_copy(whole.at[:, pl.ds(n * chunk, chunk)], buf.at[n], sems.at[n, which])
            for which, (whole, buf) in enumerate(pieces)
        ]
        for n in range(CUTS)
    ]
    for group in copies:
        for copy in group:
            copy.start()
    a_proj = jnp.zeros((tokens, rank_dim), jnp.float32)
    g_proj = jnp.zeros((tokens, rank_dim), jnp.float32)
    for n, group in enumerate(copies):
        for copy in group:
            copy.wait()
        a_proj += mxu(act_buf[n], in_buf[n], LASTS)
        g_proj += mxu(out_buf[n], proj_buf[n], LASTS)
    g_turned = g_proj.T
    pairs = rank_dim * rank_dim // LANES
    example = lax.broadcasted_iota(jnp.int32, (local_ex, tokens), 0)
    owner = lax.broadcasted_iota(jnp.int32, (local_ex, tokens), 1) // tok_len
    own = jnp.where(example == owner, 1.0, 0.0).astype(jnp.float32)
    per_pair = LANES // rank_dim
    a_high, a_low = halves(a_proj)
    both = jnp.concatenate([a_high, a_low], axis=1)
    g_high, g_low = [half.astype(jnp.float32) for half in halves(g_turned * tok_len ** (-0.5))]

    def spread(source, part):
        picks = [source[n * per_pair + part : n * per_pair + part + 1, :] * own for n in range(pairs)]
        return jnp.concatenate(picks, axis=0).astype(jnp.bfloat16)

    parts = []
    for part in range(per_pair):
        wide = mxu(spread(g_high, part), both)
        parts.append(wide[:, :rank_dim] + wide[:, rank_dim:] + mxu(spread(g_low, part), a_high))
    grads = jnp.concatenate(parts, axis=1).astype(jnp.bfloat16)
    wide = grads.astype(jnp.float32)
    square = jnp.sum(wide * wide, axis=0, keepdims=True)
    rows = pairs * local_ex
    packed_ref[:rows, :] = grads
    row_at = lax.broadcasted_iota(jnp.int32, (local_ex, LANES), 0)
    first = square.astype(jnp.bfloat16).astype(jnp.float32)
    second = (square - first).astype(jnp.bfloat16).astype(jnp.float32)
    third = square - first - second
    coded = jnp.where(row_at == 0, first, jnp.where(row_at == 1, second, jnp.where(row_at == 2, third, 0.0)))
    packed_ref[rows:, :] = coded.astype(jnp.bfloat16)


def project(activations, out_grads, proj_in, proj_out):
    local_ex, tok_len, model_dim = activations.shape
    rank_dim = proj_in.shape[1]
    tokens = local_ex * tok_len
    pairs = rank_dim * rank_dim // LANES
    hbm = pl.BlockSpec(memory_space=pltpu.HBM)
    packed = pl.pallas_call(
        functools.partial(project_kernel, local_ex=local_ex, tok_len=tok_len),
        in_specs=[hbm] * 4,
        out_specs=pl.BlockSpec(memory_space=pltpu.VMEM),
        out_shape=jax.ShapeDtypeStruct(((pairs + 1) * local_ex, LANES), jnp.bfloat16),
        scratch_shapes=[
            pltpu.VMEM((CUTS, tokens, model_dim // CUTS), jnp.bfloat16),
            pltpu.VMEM((CUTS, tokens, model_dim // CUTS), jnp.bfloat16),
            pltpu.VMEM((CUTS, rank_dim, model_dim // CUTS), jnp.bfloat16),
            pltpu.VMEM((CUTS, rank_dim, model_dim // CUTS), jnp.bfloat16),
            pltpu.SemaphoreType.DMA((CUTS, 4)),
        ],
        compiler_params=pltpu.CompilerParams(vmem_limit_bytes=32 * 2**20),
        name="project",
    )(
        *[
            pltpu.with_memory_space_constraint(whole, pltpu.HBM)
            for whole in (
                activations.reshape(tokens, model_dim),
                out_grads.reshape(tokens, model_dim),
                proj_in.T,
                proj_out.T,
            )
        ]
    )
    return packed.reshape(pairs + 1, local_ex, LANES)


def eliminate(work_ref, done_ref, fillers):
    tiles = BOTH // LANES
    groups = STRIP // SUB
    sub_at = lax.broadcasted_iota(jnp.int32, (SUB, LANES), 0)
    lane_at = lax.broadcasted_iota(jnp.int32, (SUB, LANES), 1)
    for start in range(0, BOTH, STRIP):
        here = start // LANES
        live = list(range(here, tiles)) + list(range(tiles, tiles + here + 1))
        rows = [
            {t: work_ref[start + g * SUB : start + (g + 1) * SUB, t * LANES : (t + 1) * LANES] for t in live}
            for g in range(groups)
        ]
        roots = []

        def spread(block, low, high):
            lane = start % LANES + block * SUB
            return [
                {
                    g: jnp.broadcast_to(rows[g][here][:, lane + m : lane + m + 1], (SUB, LANES))
                    for g in range(low, high)
                }
                for m in range(SUB)
            ]

        cols = spread(0, 0, groups)
        for block in range(groups):
            near = min(block + 1 + AHEAD, groups)
            ahead = spread(block + 1, block + 1, near) if block + 1 < groups else None
            pivots = jnp.ones((SUB, LANES), jnp.float32)
            inverses = []
            for j in range(SUB):
                lead = cols[j]
                pivot = lead[block][j : j + 1, :]
                inverse = 1.0 / pivot
                inverses.append(inverse)
                pivots = jnp.where(sub_at == j, pivot, pivots)
                near_scaled = lead[block] * inverse
                next_scaled = lead[block + 1] * inverse if ahead is not None else None
                for m in range(j + 1, SUB):
                    factor = near_scaled[m : m + 1, :]
                    for g in cols[m]:
                        cols[m][g] = cols[m][g] - lead[g] * factor
                if ahead is not None:
                    for m in range(SUB):
                        factor = next_scaled[m : m + 1, :]
                        for g in ahead[m]:
                            ahead[m][g] = ahead[m][g] - lead[g] * factor
                scaled = {t: rows[block][t][j : j + 1, :] * inverse for t in live}
                for g in range(block, groups):
                    weight = lead[g]
                    if g == block:
                        if j == SUB - 1:
                            continue
                        weight = jnp.where(sub_at > j, weight, 0.0)
                    for t in live:
                        rows[g][t] = rows[g][t] - weight * scaled[t]
            roots.append(lax.rsqrt(pivots))
            for filler in itertools.islice(fillers, FILL):
                filler()
            if ahead is not None:
                cols = ahead
                for m, late in enumerate(spread(block + 1, near, groups)):
                    cols[m].update(late)
        for g in range(groups):
            for t in range(2 * tiles):
                at = slice(start + g * SUB, start + (g + 1) * SUB), slice(t * LANES, (t + 1) * LANES)
                if t not in live:
                    done_ref[at] = jnp.zeros((SUB, LANES), jnp.float32)
                    continue
                value = rows[g][t] * roots[g]
                if t == here:
                    value = jnp.where(lane_at + t * LANES >= sub_at + start + g * SUB, value, 0.0)
                done_ref[at] = value
        beyond = start + STRIP
        if beyond < BOTH:
            first = beyond // LANES * LANES
            last = BOTH + -(-beyond // LANES) * LANES
            right = done_ref[start:beyond, first:last]
            rh, rm, rl = thirds(right)
            cuts = [beyond, beyond + STRIP] + ([BOTH] if beyond + STRIP < BOTH else [])
            for low, high in zip(cuts[:-1], cuts[1:]):
                left = done_ref[start:beyond, low:high]
                lh, lm, ll = thirds(left)
                work_ref[low:high, first:last] -= mxu(
                    jnp.concatenate([lh, lh, lm, lh, ll, lm], axis=0),
                    jnp.concatenate([rh, rm, rh, rl, rh, rm], axis=0),
                    FIRSTS,
                )


def fisher_kernel(
    place_ref, level_ref, panel_level_ref, *refs, sources, total_ex, feats
):
    arrived = refs[:sources]
    out_ref, g_panel, g_row, g_col, turned, work, done, weights, held, sems = refs[sources:]
    row_at, col_at = place_ref[0], place_ref[1]
    here = arrived[0].shape[1]
    row_span, col_span = held.shape
    row_blocks, col_blocks, panel_blocks = row_span // LANES, col_span // LANES, BOTH // LANES
    examples = sources * here
    col_base = 2 * row_blocks
    panel_base = col_base + col_blocks
    row_base = lax.rem(row_at, 2) * row_blocks

    def gather(target, base, blocks, n):
        for b in range(blocks):
            target[n * here : (n + 1) * here, b * LANES : (b + 1) * LANES] = arrived[n][base + b]

    total = jnp.zeros((here, LANES), jnp.float32)
    for n in range(sources):
        gather(g_panel, panel_base, panel_blocks, n)
        total += arrived[n][panel_base + panel_blocks].astype(jnp.float32)
    total_sq = jnp.sum(jnp.sum(total, axis=0, keepdims=True), axis=1, keepdims=True)
    damping = damp_coef * total_sq / (total_ex * feats)
    panel = g_panel[...]
    rows_at = lax.broadcasted_iota(jnp.int32, (BOTH, BOTH), 0)
    cols_at = lax.broadcasted_iota(jnp.int32, (BOTH, BOTH), 1)
    same = rows_at == cols_at
    work[:, :BOTH] = mxu(panel, panel, FIRSTS) * (1.0 / total_ex) + jnp.where(
        same, damping * panel_level_ref[...], 0.0
    )
    work[:, BOTH:] = jnp.where(same, 1.0, 0.0)

    def turn(first):
        turned[first : first + LANES, :] = g_row[:, first : first + LANES].T

    fillers = iter(
        [functools.partial(gather, g_row, row_base, row_blocks, n) for n in range(sources)]
        + [functools.partial(turn, first) for first in range(0, row_span, LANES)]
        + [functools.partial(gather, g_col, col_base, col_blocks, n) for n in range(sources)]
    )
    eliminate(work, done, fillers)
    for filler in fillers:
        filler()

    mixed = mxu(
        jnp.concatenate([panel, panel], axis=1), jnp.concatenate(halves(done[:, BOTH:]), axis=1), LASTS
    )
    y_high, y_low = halves(mixed)
    outer = mxu(
        jnp.concatenate([y_high, y_high, y_low], axis=1), jnp.concatenate([y_high, y_low, y_high], axis=1), LASTS
    )
    ex_rows = lax.broadcasted_iota(jnp.int32, outer.shape, 0)
    ex_cols = lax.broadcasted_iota(jnp.int32, outer.shape, 1)
    mix = (jnp.where(ex_rows == ex_cols, 1.0, 0.0) - outer * (1.0 / total_ex)) * (1.0 / total_ex)
    both = jnp.concatenate(halves(mix), axis=0)
    chunks = [slice(first, first + BOTH) for first in reversed(range(0, col_span, BOTH))]
    for lanes in chunks:
        value = mxu(both, g_col[:, lanes])
        value = value[:examples] + value[examples:]
        if lanes.start == 0:
            value = jnp.where(col_at == 0, mixed * (1.0 / total_ex), value)
        weights[:examples, lanes], weights[examples:, lanes] = halves(value)

    lower = done[:, :BOTH].T
    eye = lax.broadcasted_iota(jnp.int32, (LANES, LANES), 0) == lax.broadcasted_iota(
        jnp.int32, (LANES, LANES), 1
    )
    left = jnp.concatenate([turned[...], turned[...]], axis=1)
    copies = []
    for n, lanes in enumerate(chunks):
        value = mxu(left, weights[:, lanes])
        special = jnp.where(col_at == 0, lower, 0.0) if lanes.start == 0 else jnp.zeros_like(lower)
        held[:BOTH, lanes] = jnp.where(row_at == 0, special, value[:BOTH])
        if row_span > BOTH:
            held[BOTH:, lanes] = value[BOTH:]
        for b in range(panel_blocks):
            start = lanes.start + b * LANES
            block = col_at * col_blocks + start // LANES - row_at * row_blocks
            inside = (block >= 0) & (block < row_blocks)
            if lanes.start == 0:
                inside = inside & (col_at > 0)
            rows = pl.ds(pl.multiple_of(jnp.clip(block, 0, row_blocks - 1) * LANES, LANES), LANES)
            held[rows, start : start + LANES] += jnp.where(
                eye & inside, level_ref[:, start : start + LANES] * damping, 0.0
            )
        copy = pltpu.make_async_copy(held.at[:, lanes], out_ref.at[:, lanes], sems.at[n])
        copy.start()
        copies.append(copy)
    for copy in copies:
        copy.wait()


def fisher(place, col_levels, panel_levels, arrived, row_blocks, col_blocks, total_ex, feats):
    row_span, col_span = row_blocks * LANES, col_blocks * LANES
    sources = len(arrived)
    vmem = pl.BlockSpec(memory_space=pltpu.VMEM)
    return pl.pallas_call(
        functools.partial(fisher_kernel, sources=sources, total_ex=total_ex, feats=feats),
        in_specs=[pl.BlockSpec(memory_space=pltpu.SMEM)] + [vmem] * (2 + sources),
        out_specs=pl.BlockSpec(memory_space=pltpu.HBM),
        out_shape=jax.ShapeDtypeStruct((row_span, col_span), jnp.float32),
        scratch_shapes=[
            pltpu.VMEM((total_ex, BOTH), jnp.bfloat16),
            pltpu.VMEM((total_ex, row_span), jnp.bfloat16),
            pltpu.VMEM((total_ex, col_span), jnp.bfloat16),
            pltpu.VMEM((row_span, total_ex), jnp.bfloat16),
            pltpu.VMEM((BOTH, 2 * BOTH), jnp.float32),
            pltpu.VMEM((BOTH, 2 * BOTH), jnp.float32),
            pltpu.VMEM((2 * total_ex, col_span), jnp.bfloat16),
            pltpu.VMEM((row_span, col_span), jnp.float32),
            pltpu.SemaphoreType.DMA((col_span // BOTH,)),
        ],
        compiler_params=pltpu.CompilerParams(vmem_limit_bytes=32 * 2**20),
        name="fisher",
    )(place, col_levels, panel_levels, *arrived)


def swap(block, axis, mask):
    size = lax.axis_size(axis)
    return lax.ppermute(block, axis, [(n, n ^ mask) for n in range(size)])


def shards(activations, out_grads, proj_in, proj_out, damp_level):
    local_ex = activations.shape[0]
    feats = proj_in.shape[1] * proj_out.shape[1]
    n_rows = lax.axis_size("row")
    n_cols = lax.axis_size("col")
    total_ex = local_ex * n_rows * n_cols
    row_at = lax.axis_index("row")
    col_at = lax.axis_index("col")
    blocks = feats // LANES
    row_blocks = blocks // n_rows
    col_blocks = blocks // n_cols

    levels = damp_level.astype(jnp.float32).reshape(1, feats)
    col_levels = lax.dynamic_slice_in_dim(levels, col_at * col_blocks * LANES, col_blocks * LANES, axis=1)
    place = jnp.stack([row_at, col_at]).astype(jnp.int32)

    packed = project(activations, out_grads, proj_in, proj_out)
    along = [packed] + [swap(packed, "col", mask) for mask in range(n_cols - 1, 0, -1)]
    line = jnp.concatenate(along, axis=1)

    common = [
        lax.dynamic_slice_in_dim(line, col_at * col_blocks, col_blocks),
        line[: BOTH // LANES],
        line[blocks:],
    ]
    pairs = n_rows // 2
    pair_at = row_at // 2

    def bundle(pair):
        wanted = lax.dynamic_slice_in_dim(line, pair * 2 * row_blocks, 2 * row_blocks)
        return jnp.concatenate([wanted] + common)

    got = [bundle(pair_at)] + [swap(bundle(pair_at ^ mask), "row", 2 * mask) for mask in range(1, pairs)]
    arrived = got + [swap(piece, "row", 1) for piece in got]
    return fisher(
        place, col_levels, levels[:, :BOTH], arrived, row_blocks, col_blocks, total_ex, feats
    )


def solution(mesh):
    return jax.shard_map(
        shards,
        mesh=mesh,
        in_specs=(P(("row", "col"), None, None), P(("row", "col"), None, None), P(), P(), P()),
        out_specs=P("row", "col"),
        check_vma=False,
    )
```

```python
import functools
import itertools

import jax
import jax.numpy as jnp
from jax import lax
from jax.experimental import pallas as pl
from jax.experimental.pallas import tpu as pltpu
from jax.sharding import PartitionSpec as P

PANEL = 128
BOTH = 2 * PANEL
LANES = 128
SUB = 8
STRIP = 64
AHEAD = 1
FILL = 2

damp_coef = 0.25

HIGHEST = lax.Precision.HIGHEST
FIRSTS = (((0,), (0,)), ((), ()))
LASTS = (((1,), (1,)), ((), ()))
PLAIN = (((1,), (0,)), ((), ()))


def mxu(left, right, dims=PLAIN):
    return lax.dot_general(left, right, dims, preferred_element_type=jnp.float32)


def halves(value):
    high = value.astype(jnp.bfloat16)
    return high, (value - high.astype(jnp.float32)).astype(jnp.bfloat16)


CUTS = 8


def thirds(value):
    high = value.astype(jnp.bfloat16)
    return (high, *halves(value - high.astype(jnp.float32)))


def project_kernel(
    act_hbm, out_hbm, in_hbm, proj_hbm, packed_ref, act_buf, out_buf, in_buf, proj_buf, sems, *, local_ex, tok_len
):
    _, tokens, chunk = act_buf.shape
    rank_dim = in_buf.shape[1]
    pieces = (in_hbm, in_buf), (act_hbm, act_buf), (proj_hbm, proj_buf), (out_hbm, out_buf)
    copies = [
        [
            pltpu.make_async_copy(whole.at[:, pl.ds(n * chunk, chunk)], buf.at[n], sems.at[n, which])
            for which, (whole, buf) in enumerate(pieces)
        ]
        for n in range(CUTS)
    ]
    for group in copies:
        for copy in group:
            copy.start()
    a_proj = jnp.zeros((tokens, rank_dim), jnp.float32)
    g_proj = jnp.zeros((tokens, rank_dim), jnp.float32)
    for n, group in enumerate(copies):
        for copy in group:
            copy.wait()
        a_proj += mxu(act_buf[n], in_buf[n], LASTS)
        g_proj += mxu(out_buf[n], proj_buf[n], LASTS)
    g_turned = g_proj.T
    pairs = rank_dim * rank_dim // LANES
    example = lax.broadcasted_iota(jnp.int32, (local_ex, tokens), 0)
    owner = lax.broadcasted_iota(jnp.int32, (local_ex, tokens), 1) // tok_len
    own = jnp.where(example == owner, 1.0, 0.0).astype(jnp.float32)
    per_pair = LANES // rank_dim
    a_high, a_low = halves(a_proj)
    both = jnp.concatenate([a_high, a_low], axis=1)
    g_high, g_low = [half.astype(jnp.float32) for half in halves(g_turned * tok_len ** (-0.5))]

    def spread(source, part):
        picks = [source[n * per_pair + part : n * per_pair + part + 1, :] * own for n in range(pairs)]
        return jnp.concatenate(picks, axis=0).astype(jnp.bfloat16)

    parts = []
    for part in range(per_pair):
        wide = mxu(spread(g_high, part), both)
        parts.append(wide[:, :rank_dim] + wide[:, rank_dim:] + mxu(spread(g_low, part), a_high))
    grads = jnp.concatenate(parts, axis=1).astype(jnp.bfloat16)
    wide = grads.astype(jnp.float32)
    square = jnp.sum(wide * wide, axis=0, keepdims=True)
    rows = pairs * local_ex
    packed_ref[:rows, :] = grads
    row_at = lax.broadcasted_iota(jnp.int32, (local_ex, LANES), 0)
    first = square.astype(jnp.bfloat16).astype(jnp.float32)
    second = (square - first).astype(jnp.bfloat16).astype(jnp.float32)
    third = square - first - second
    coded = jnp.where(row_at == 0, first, jnp.where(row_at == 1, second, jnp.where(row_at == 2, third, 0.0)))
    packed_ref[rows:, :] = coded.astype(jnp.bfloat16)


def project(activations, out_grads, proj_in, proj_out):
    local_ex, tok_len, model_dim = activations.shape
    rank_dim = proj_in.shape[1]
    tokens = local_ex * tok_len
    pairs = rank_dim * rank_dim // LANES
    hbm = pl.BlockSpec(memory_space=pltpu.HBM)
    packed = pl.pallas_call(
        functools.partial(project_kernel, local_ex=local_ex, tok_len=tok_len),
        in_specs=[hbm] * 4,
        out_specs=pl.BlockSpec(memory_space=pltpu.VMEM),
        out_shape=jax.ShapeDtypeStruct(((pairs + 1) * local_ex, LANES), jnp.bfloat16),
        scratch_shapes=[
            pltpu.VMEM((CUTS, tokens, model_dim // CUTS), jnp.bfloat16),
            pltpu.VMEM((CUTS, tokens, model_dim // CUTS), jnp.bfloat16),
            pltpu.VMEM((CUTS, rank_dim, model_dim // CUTS), jnp.bfloat16),
            pltpu.VMEM((CUTS, rank_dim, model_dim // CUTS), jnp.bfloat16),
            pltpu.SemaphoreType.DMA((CUTS, 4)),
        ],
        compiler_params=pltpu.CompilerParams(vmem_limit_bytes=32 * 2**20),
        name="project",
    )(
        *[
            pltpu.with_memory_space_constraint(whole, pltpu.HBM)
            for whole in (
                activations.reshape(tokens, model_dim),
                out_grads.reshape(tokens, model_dim),
                proj_in.T,
                proj_out.T,
            )
        ]
    )
    return packed.reshape(pairs + 1, local_ex, LANES)


def eliminate(work_ref, done_ref, fillers):
    tiles = BOTH // LANES
    groups = STRIP // SUB
    sub_at = lax.broadcasted_iota(jnp.int32, (SUB, LANES), 0)
    lane_at = lax.broadcasted_iota(jnp.int32, (SUB, LANES), 1)
    for start in range(0, BOTH, STRIP):
        here = start // LANES
        live = list(range(here, tiles)) + list(range(tiles, tiles + here + 1))
        rows = [
            {t: work_ref[start + g * SUB : start + (g + 1) * SUB, t * LANES : (t + 1) * LANES] for t in live}
            for g in range(groups)
        ]
        roots = []

        def spread(block, low, high):
            lane = start % LANES + block * SUB
            return [
                {
                    g: jnp.broadcast_to(rows[g][here][:, lane + m : lane + m + 1], (SUB, LANES))
                    for g in range(low, high)
                }
                for m in range(SUB)
            ]

        cols = spread(0, 0, groups)
        for block in range(groups):
            near = min(block + 1 + AHEAD, groups)
            ahead = spread(block + 1, block + 1, near) if block + 1 < groups else None
            pivots = jnp.ones((SUB, LANES), jnp.float32)
            inverses = []
            for j in range(SUB):
                lead = cols[j]
                pivot = lead[block][j : j + 1, :]
                inverse = 1.0 / pivot
                inverses.append(inverse)
                pivots = jnp.where(sub_at == j, pivot, pivots)
                near_scaled = lead[block] * inverse
                next_scaled = lead[block + 1] * inverse if ahead is not None else None
                for m in range(j + 1, SUB):
                    factor = near_scaled[m : m + 1, :]
                    for g in cols[m]:
                        cols[m][g] = cols[m][g] - lead[g] * factor
                if ahead is not None:
                    for m in range(SUB):
                        factor = next_scaled[m : m + 1, :]
                        for g in ahead[m]:
                            ahead[m][g] = ahead[m][g] - lead[g] * factor
                scaled = {t: rows[block][t][j : j + 1, :] * inverse for t in live}
                for g in range(block, groups):
                    weight = lead[g]
                    if g == block:
                        if j == SUB - 1:
                            continue
                        weight = jnp.where(sub_at > j, weight, 0.0)
                    for t in live:
                        rows[g][t] = rows[g][t] - weight * scaled[t]
            roots.append(lax.rsqrt(pivots))
            for filler in itertools.islice(fillers, FILL):
                filler()
            if ahead is not None:
                cols = ahead
                for m, late in enumerate(spread(block + 1, near, groups)):
                    cols[m].update(late)
        for g in range(groups):
            for t in range(2 * tiles):
                at = slice(start + g * SUB, start + (g + 1) * SUB), slice(t * LANES, (t + 1) * LANES)
                if t not in live:
                    done_ref[at] = jnp.zeros((SUB, LANES), jnp.float32)
                    continue
                value = rows[g][t] * roots[g]
                if t == here:
                    value = jnp.where(lane_at + t * LANES >= sub_at + start + g * SUB, value, 0.0)
                done_ref[at] = value
        beyond = start + STRIP
        if beyond < BOTH:
            first = beyond // LANES * LANES
            last = BOTH + -(-beyond // LANES) * LANES
            right = done_ref[start:beyond, first:last]
            rh, rm, rl = thirds(right)
            cuts = [beyond, beyond + STRIP] + ([BOTH] if beyond + STRIP < BOTH else [])
            for low, high in zip(cuts[:-1], cuts[1:]):
                left = done_ref[start:beyond, low:high]
                lh, lm, ll = thirds(left)
                work_ref[low:high, first:last] -= mxu(
                    jnp.concatenate([lh, lh, lm, lh, ll, lm], axis=0),
                    jnp.concatenate([rh, rm, rh, rl, rh, rm], axis=0),
                    FIRSTS,
                )


def fisher_kernel(
    place_ref, level_ref, panel_level_ref, *refs, sources, total_ex, feats
):
    arrived = refs[:sources]
    out_ref, g_panel, g_row, g_col, turned, work, done, weights, held, sems = refs[sources:]
    row_at, col_at = place_ref[0], place_ref[1]
    here = arrived[0].shape[1]
    row_span, col_span = held.shape
    row_blocks, col_blocks, panel_blocks = row_span // LANES, col_span // LANES, BOTH // LANES
    examples = sources * here
    col_base = 2 * row_blocks
    panel_base = col_base + col_blocks
    row_base = lax.rem(row_at, 2) * row_blocks

    def gather(target, base, blocks, n):
        for b in range(blocks):
            target[n * here : (n + 1) * here, b * LANES : (b + 1) * LANES] = arrived[n][base + b]

    total = jnp.zeros((here, LANES), jnp.float32)
    for n in range(sources):
        gather(g_panel, panel_base, panel_blocks, n)
        total += arrived[n][panel_base + panel_blocks].astype(jnp.float32)
    total_sq = jnp.sum(jnp.sum(total, axis=0, keepdims=True), axis=1, keepdims=True)
    damping = damp_coef * total_sq / (total_ex * feats)
    panel = g_panel[...]
    rows_at = lax.broadcasted_iota(jnp.int32, (BOTH, BOTH), 0)
    cols_at = lax.broadcasted_iota(jnp.int32, (BOTH, BOTH), 1)
    same = rows_at == cols_at
    work[:, :BOTH] = mxu(panel, panel, FIRSTS) * (1.0 / total_ex) + jnp.where(
        same, damping * panel_level_ref[...], 0.0
    )
    work[:, BOTH:] = jnp.where(same, 1.0, 0.0)

    def turn(first):
        turned[first : first + LANES, :] = g_row[:, first : first + LANES].T

    fillers = iter(
        [functools.partial(gather, g_row, row_base, row_blocks, n) for n in range(sources)]
        + [functools.partial(turn, first) for first in range(0, row_span, LANES)]
        + [functools.partial(gather, g_col, col_base, col_blocks, n) for n in range(sources)]
    )
    eliminate(work, done, fillers)
    for filler in fillers:
        filler()

    mixed = mxu(
        jnp.concatenate([panel, panel], axis=1), jnp.concatenate(halves(done[:, BOTH:]), axis=1), LASTS
    )
    y_high, y_low = halves(mixed)
    outer = mxu(
        jnp.concatenate([y_high, y_high, y_low], axis=1), jnp.concatenate([y_high, y_low, y_high], axis=1), LASTS
    )
    ex_rows = lax.broadcasted_iota(jnp.int32, outer.shape, 0)
    ex_cols = lax.broadcasted_iota(jnp.int32, outer.shape, 1)
    mix = (jnp.where(ex_rows == ex_cols, 1.0, 0.0) - outer * (1.0 / total_ex)) * (1.0 / total_ex)
    both = jnp.concatenate(halves(mix), axis=0)
    chunks = [slice(first, first + BOTH) for first in reversed(range(0, col_span, BOTH))]
    for lanes in chunks:
        value = mxu(both, g_col[:, lanes])
        value = value[:examples] + value[examples:]
        if lanes.start == 0:
            value = jnp.where(col_at == 0, mixed * (1.0 / total_ex), value)
        weights[:examples, lanes], weights[examples:, lanes] = halves(value)

    lower = done[:, :BOTH].T
    eye = lax.broadcasted_iota(jnp.int32, (LANES, LANES), 0) == lax.broadcasted_iota(
        jnp.int32, (LANES, LANES), 1
    )
    left = jnp.concatenate([turned[...], turned[...]], axis=1)
    copies = []
    for n, lanes in enumerate(chunks):
        value = mxu(left, weights[:, lanes])
        special = jnp.where(col_at == 0, lower, 0.0) if lanes.start == 0 else jnp.zeros_like(lower)
        held[:BOTH, lanes] = jnp.where(row_at == 0, special, value[:BOTH])
        if row_span > BOTH:
            held[BOTH:, lanes] = value[BOTH:]
        for b in range(panel_blocks):
            start = lanes.start + b * LANES
            block = col_at * col_blocks + start // LANES - row_at * row_blocks
            inside = (block >= 0) & (block < row_blocks)
            if lanes.start == 0:
                inside = inside & (col_at > 0)
            rows = pl.ds(pl.multiple_of(jnp.clip(block, 0, row_blocks - 1) * LANES, LANES), LANES)
            held[rows, start : start + LANES] += jnp.where(
                eye & inside, level_ref[:, start : start + LANES] * damping, 0.0
            )
        copy = pltpu.make_async_copy(held.at[:, lanes], out_ref.at[:, lanes], sems.at[n])
        copy.start()
        copies.append(copy)
    for copy in copies:
        copy.wait()


def fisher(place, col_levels, panel_levels, arrived, row_blocks, col_blocks, total_ex, feats):
    row_span, col_span = row_blocks * LANES, col_blocks * LANES
    sources = len(arrived)
    vmem = pl.BlockSpec(memory_space=pltpu.VMEM)
    return pl.pallas_call(
        functools.partial(fisher_kernel, sources=sources, total_ex=total_ex, feats=feats),
        in_specs=[pl.BlockSpec(memory_space=pltpu.SMEM)] + [vmem] * (2 + sources),
        out_specs=pl.BlockSpec(memory_space=pltpu.HBM),
        out_shape=jax.ShapeDtypeStruct((row_span, col_span), jnp.float32),
        scratch_shapes=[
            pltpu.VMEM((total_ex, BOTH), jnp.bfloat16),
            pltpu.VMEM((total_ex, row_span), jnp.bfloat16),
            pltpu.VMEM((total_ex, col_span), jnp.bfloat16),
            pltpu.VMEM((row_span, total_ex), jnp.bfloat16),
            pltpu.VMEM((BOTH, 2 * BOTH), jnp.float32),
            pltpu.VMEM((BOTH, 2 * BOTH), jnp.float32),
            pltpu.VMEM((2 * total_ex, col_span), jnp.bfloat16),
            pltpu.VMEM((row_span, col_span), jnp.float32),
            pltpu.SemaphoreType.DMA((col_span // BOTH,)),
        ],
        compiler_params=pltpu.CompilerParams(vmem_limit_bytes=32 * 2**20),
        name="fisher",
    )(place, col_levels, panel_levels, *arrived)


def swap(block, axis, mask):
    size = lax.axis_size(axis)
    return lax.ppermute(block, axis, [(n, n ^ mask) for n in range(size)])


def shards(activations, out_grads, proj_in, proj_out, damp_level):
    local_ex = activations.shape[0]
    feats = proj_in.shape[1] * proj_out.shape[1]
    n_rows = lax.axis_size("row")
    n_cols = lax.axis_size("col")
    total_ex = local_ex * n_rows * n_cols
    row_at = lax.axis_index("row")
    col_at = lax.axis_index("col")
    blocks = feats // LANES
    row_blocks = blocks // n_rows
    col_blocks = blocks // n_cols

    levels = damp_level.astype(jnp.float32).reshape(1, feats)
    col_levels = lax.dynamic_slice_in_dim(levels, col_at * col_blocks * LANES, col_blocks * LANES, axis=1)
    place = jnp.stack([row_at, col_at]).astype(jnp.int32)

    packed = project(activations, out_grads, proj_in, proj_out)
    order = [*range(1, min(2, n_cols)), *range(n_cols - 1, 1, -1)]
    along = [packed] + [swap(packed, "col", mask) for mask in order]
    line = jnp.concatenate(along, axis=1)

    common = [
        lax.dynamic_slice_in_dim(line, col_at * col_blocks, col_blocks),
        line[: BOTH // LANES],
        line[blocks:],
    ]
    pairs = n_rows // 2
    pair_at = row_at // 2

    def bundle(pair):
        wanted = lax.dynamic_slice_in_dim(line, pair * 2 * row_blocks, 2 * row_blocks)
        return jnp.concatenate([wanted] + common)

    got = [bundle(pair_at)] + [swap(bundle(pair_at ^ mask), "row", 2 * mask) for mask in range(1, pairs)]
    arrived = got + [swap(piece, "row", 1) for piece in got]
    return fisher(
        place, col_levels, levels[:, :BOTH], arrived, row_blocks, col_blocks, total_ex, feats
    )


def solution(mesh):
    return jax.shard_map(
        shards,
        mesh=mesh,
        in_specs=(P(("row", "col"), None, None), P(("row", "col"), None, None), P(), P(), P()),
        out_specs=P("row", "col"),
        check_vma=False,
    )
```

```python
import functools
import itertools

import jax
import jax.numpy as jnp
from jax import lax
from jax.experimental import pallas as pl
from jax.experimental.pallas import tpu as pltpu
from jax.sharding import PartitionSpec as P

PANEL = 128
BOTH = 2 * PANEL
LANES = 128
SUB = 8
STRIP = 64
AHEAD = 1
FILL = 2

damp_coef = 0.25

HIGHEST = lax.Precision.HIGHEST
FIRSTS = (((0,), (0,)), ((), ()))
LASTS = (((1,), (1,)), ((), ()))
PLAIN = (((1,), (0,)), ((), ()))


def mxu(left, right, dims=PLAIN):
    return lax.dot_general(left, right, dims, preferred_element_type=jnp.float32)


def halves(value):
    high = value.astype(jnp.bfloat16)
    return high, (value - high.astype(jnp.float32)).astype(jnp.bfloat16)


CUTS = 8


def thirds(value):
    high = value.astype(jnp.bfloat16)
    return (high, *halves(value - high.astype(jnp.float32)))


def project_kernel(
    act_hbm, out_hbm, in_hbm, proj_hbm, packed_ref, act_buf, out_buf, in_buf, proj_buf, sems, *, local_ex, tok_len
):
    _, tokens, chunk = act_buf.shape
    rank_dim = in_buf.shape[1]
    pieces = (in_hbm, in_buf), (act_hbm, act_buf), (proj_hbm, proj_buf), (out_hbm, out_buf)
    copies = [
        [
            pltpu.make_async_copy(whole.at[:, pl.ds(n * chunk, chunk)], buf.at[n], sems.at[n, which])
            for which, (whole, buf) in enumerate(pieces)
        ]
        for n in range(CUTS)
    ]
    for group in copies:
        for copy in group:
            copy.start()
    a_proj = jnp.zeros((tokens, rank_dim), jnp.float32)
    g_proj = jnp.zeros((tokens, rank_dim), jnp.float32)
    for n, group in enumerate(copies):
        for copy in group:
            copy.wait()
        a_proj += mxu(act_buf[n], in_buf[n], LASTS)
        g_proj += mxu(out_buf[n], proj_buf[n], LASTS)
    g_turned = g_proj.T
    pairs = rank_dim * rank_dim // LANES
    example = lax.broadcasted_iota(jnp.int32, (local_ex, tokens), 0)
    owner = lax.broadcasted_iota(jnp.int32, (local_ex, tokens), 1) // tok_len
    own = jnp.where(example == owner, 1.0, 0.0).astype(jnp.float32)
    per_pair = LANES // rank_dim
    a_high, a_low = halves(a_proj)
    both = jnp.concatenate([a_high, a_low], axis=1)
    g_high, g_low = [half.astype(jnp.float32) for half in halves(g_turned * tok_len ** (-0.5))]

    def spread(source, part):
        picks = [source[n * per_pair + part : n * per_pair + part + 1, :] * own for n in range(pairs)]
        return jnp.concatenate(picks, axis=0).astype(jnp.bfloat16)

    parts = []
    for part in range(per_pair):
        wide = mxu(spread(g_high, part), both)
        parts.append(wide[:, :rank_dim] + wide[:, rank_dim:] + mxu(spread(g_low, part), a_high))
    grads = jnp.concatenate(parts, axis=1).astype(jnp.bfloat16)
    wide = grads.astype(jnp.float32)
    square = jnp.sum(wide * wide, axis=0, keepdims=True)
    rows = pairs * local_ex
    packed_ref[:rows, :] = grads
    row_at = lax.broadcasted_iota(jnp.int32, (local_ex, LANES), 0)
    first = square.astype(jnp.bfloat16).astype(jnp.float32)
    second = (square - first).astype(jnp.bfloat16).astype(jnp.float32)
    third = square - first - second
    coded = jnp.where(row_at == 0, first, jnp.where(row_at == 1, second, jnp.where(row_at == 2, third, 0.0)))
    packed_ref[rows:, :] = coded.astype(jnp.bfloat16)


def project(activations, out_grads, proj_in, proj_out):
    local_ex, tok_len, model_dim = activations.shape
    rank_dim = proj_in.shape[1]
    tokens = local_ex * tok_len
    pairs = rank_dim * rank_dim // LANES
    hbm = pl.BlockSpec(memory_space=pltpu.HBM)
    packed = pl.pallas_call(
        functools.partial(project_kernel, local_ex=local_ex, tok_len=tok_len),
        in_specs=[hbm] * 4,
        out_specs=pl.BlockSpec(memory_space=pltpu.VMEM),
        out_shape=jax.ShapeDtypeStruct(((pairs + 1) * local_ex, LANES), jnp.bfloat16),
        scratch_shapes=[
            pltpu.VMEM((CUTS, tokens, model_dim // CUTS), jnp.bfloat16),
            pltpu.VMEM((CUTS, tokens, model_dim // CUTS), jnp.bfloat16),
            pltpu.VMEM((CUTS, rank_dim, model_dim // CUTS), jnp.bfloat16),
            pltpu.VMEM((CUTS, rank_dim, model_dim // CUTS), jnp.bfloat16),
            pltpu.SemaphoreType.DMA((CUTS, 4)),
        ],
        compiler_params=pltpu.CompilerParams(vmem_limit_bytes=32 * 2**20),
        name="project",
    )(
        *[
            pltpu.with_memory_space_constraint(whole, pltpu.HBM)
            for whole in (
                activations.reshape(tokens, model_dim),
                out_grads.reshape(tokens, model_dim),
                proj_in.T,
                proj_out.T,
            )
        ]
    )
    return packed.reshape(pairs + 1, local_ex, LANES)


def eliminate(work_ref, done_ref, fillers):
    tiles = BOTH // LANES
    groups = STRIP // SUB
    sub_at = lax.broadcasted_iota(jnp.int32, (SUB, LANES), 0)
    lane_at = lax.broadcasted_iota(jnp.int32, (SUB, LANES), 1)
    for start in range(0, BOTH, STRIP):
        here = start // LANES
        live = list(range(here, tiles)) + list(range(tiles, tiles + here + 1))
        rows = [
            {t: work_ref[start + g * SUB : start + (g + 1) * SUB, t * LANES : (t + 1) * LANES] for t in live}
            for g in range(groups)
        ]
        roots = []

        def spread(block, low, high):
            lane = start % LANES + block * SUB
            return [
                {
                    g: jnp.broadcast_to(rows[g][here][:, lane + m : lane + m + 1], (SUB, LANES))
                    for g in range(low, high)
                }
                for m in range(SUB)
            ]

        cols = spread(0, 0, groups)
        for block in range(groups):
            near = min(block + 1 + AHEAD, groups)
            ahead = spread(block + 1, block + 1, near) if block + 1 < groups else None
            pivots = jnp.ones((SUB, LANES), jnp.float32)
            inverses = []
            for j in range(SUB):
                lead = cols[j]
                pivot = lead[block][j : j + 1, :]
                inverse = 1.0 / pivot
                inverses.append(inverse)
                pivots = jnp.where(sub_at == j, pivot, pivots)
                near_scaled = lead[block] * inverse
                next_scaled = lead[block + 1] * inverse if ahead is not None else None
                for m in range(j + 1, SUB):
                    factor = near_scaled[m : m + 1, :]
                    for g in cols[m]:
                        cols[m][g] = cols[m][g] - lead[g] * factor
                if ahead is not None:
                    for m in range(SUB):
                        factor = next_scaled[m : m + 1, :]
                        for g in ahead[m]:
                            ahead[m][g] = ahead[m][g] - lead[g] * factor
                scaled = {t: rows[block][t][j : j + 1, :] * inverse for t in live}
                for g in range(block, groups):
                    weight = lead[g]
                    if g == block:
                        if j == SUB - 1:
                            continue
                        weight = jnp.where(sub_at > j, weight, 0.0)
                    for t in live:
                        rows[g][t] = rows[g][t] - weight * scaled[t]
            roots.append(lax.rsqrt(pivots))
            for filler in itertools.islice(fillers, FILL):
                filler()
            if ahead is not None:
                cols = ahead
                for m, late in enumerate(spread(block + 1, near, groups)):
                    cols[m].update(late)
        for g in range(groups):
            for t in range(2 * tiles):
                at = slice(start + g * SUB, start + (g + 1) * SUB), slice(t * LANES, (t + 1) * LANES)
                if t not in live:
                    done_ref[at] = jnp.zeros((SUB, LANES), jnp.float32)
                    continue
                value = rows[g][t] * roots[g]
                if t == here:
                    value = jnp.where(lane_at + t * LANES >= sub_at + start + g * SUB, value, 0.0)
                done_ref[at] = value
        beyond = start + STRIP
        if beyond < BOTH:
            first = beyond // LANES * LANES
            last = BOTH + -(-beyond // LANES) * LANES
            right = done_ref[start:beyond, first:last]
            rh, rm, rl = thirds(right)
            cuts = [beyond, beyond + STRIP] + ([BOTH] if beyond + STRIP < BOTH else [])
            for low, high in zip(cuts[:-1], cuts[1:]):
                left = done_ref[start:beyond, low:high]
                lh, lm, ll = thirds(left)
                work_ref[low:high, first:last] -= mxu(
                    jnp.concatenate([lh, lh, lm, lh, ll, lm], axis=0),
                    jnp.concatenate([rh, rm, rh, rl, rh, rm], axis=0),
                    FIRSTS,
                )


def fisher_kernel(
    place_ref, level_ref, panel_level_ref, *refs, sources, total_ex, feats
):
    arrived = refs[:sources]
    out_ref, g_panel, g_row, g_col, turned, work, done, weights, held, sems = refs[sources:]
    row_at, col_at = place_ref[0], place_ref[1]
    here = arrived[0].shape[1]
    row_span, col_span = held.shape
    row_blocks, col_blocks, panel_blocks = row_span // LANES, col_span // LANES, BOTH // LANES
    examples = sources * here
    col_base = 2 * row_blocks
    panel_base = col_base + col_blocks
    row_base = lax.rem(row_at, 2) * row_blocks

    def gather(target, base, blocks, n):
        for b in range(blocks):
            target[n * here : (n + 1) * here, b * LANES : (b + 1) * LANES] = arrived[n][base + b]

    total = jnp.zeros((here, LANES), jnp.float32)
    for n in range(sources):
        gather(g_panel, panel_base, panel_blocks, n)
        total += arrived[n][panel_base + panel_blocks].astype(jnp.float32)
    total_sq = jnp.sum(jnp.sum(total, axis=0, keepdims=True), axis=1, keepdims=True)
    damping = damp_coef * total_sq / (total_ex * feats)
    panel = g_panel[...]
    rows_at = lax.broadcasted_iota(jnp.int32, (BOTH, BOTH), 0)
    cols_at = lax.broadcasted_iota(jnp.int32, (BOTH, BOTH), 1)
    same = rows_at == cols_at
    work[:, :BOTH] = mxu(panel, panel, FIRSTS) * (1.0 / total_ex) + jnp.where(
        same, damping * panel_level_ref[...], 0.0
    )
    work[:, BOTH:] = jnp.where(same, 1.0, 0.0)

    def turn(first):
        turned[first : first + LANES, :] = g_row[:, first : first + LANES].T

    fillers = iter(
        [functools.partial(gather, g_row, row_base, row_blocks, n) for n in range(sources)]
        + [functools.partial(turn, first) for first in range(0, row_span, LANES)]
        + [functools.partial(gather, g_col, col_base, col_blocks, n) for n in range(sources)]
    )
    eliminate(work, done, fillers)
    for filler in fillers:
        filler()

    mixed = mxu(
        jnp.concatenate([panel, panel], axis=1), jnp.concatenate(halves(done[:, BOTH:]), axis=1), LASTS
    )
    y_high, y_low = halves(mixed)
    outer = mxu(
        jnp.concatenate([y_high, y_high, y_low], axis=1), jnp.concatenate([y_high, y_low, y_high], axis=1), LASTS
    )
    ex_rows = lax.broadcasted_iota(jnp.int32, outer.shape, 0)
    ex_cols = lax.broadcasted_iota(jnp.int32, outer.shape, 1)
    mix = (jnp.where(ex_rows == ex_cols, 1.0, 0.0) - outer * (1.0 / total_ex)) * (1.0 / total_ex)
    both = jnp.concatenate(halves(mix), axis=0)
    chunks = [slice(first, first + BOTH) for first in reversed(range(0, col_span, BOTH))]
    for lanes in chunks:
        value = mxu(both, g_col[:, lanes])
        value = value[:examples] + value[examples:]
        if lanes.start == 0:
            value = jnp.where(col_at == 0, mixed * (1.0 / total_ex), value)
        weights[:examples, lanes], weights[examples:, lanes] = halves(value)

    lower = done[:, :BOTH].T
    eye = lax.broadcasted_iota(jnp.int32, (LANES, LANES), 0) == lax.broadcasted_iota(
        jnp.int32, (LANES, LANES), 1
    )
    left = jnp.concatenate([turned[...], turned[...]], axis=1)
    copies = []
    for n, lanes in enumerate(chunks):
        value = mxu(left, weights[:, lanes])
        special = jnp.where(col_at == 0, lower, 0.0) if lanes.start == 0 else jnp.zeros_like(lower)
        held[:BOTH, lanes] = jnp.where(row_at == 0, special, value[:BOTH])
        if row_span > BOTH:
            held[BOTH:, lanes] = value[BOTH:]
        for b in range(panel_blocks):
            start = lanes.start + b * LANES
            block = col_at * col_blocks + start // LANES - row_at * row_blocks
            inside = (block >= 0) & (block < row_blocks)
            if lanes.start == 0:
                inside = inside & (col_at > 0)
            rows = pl.ds(pl.multiple_of(jnp.clip(block, 0, row_blocks - 1) * LANES, LANES), LANES)
            held[rows, start : start + LANES] += jnp.where(
                eye & inside, level_ref[:, start : start + LANES] * damping, 0.0
            )
        copy = pltpu.make_async_copy(held.at[:, lanes], out_ref.at[:, lanes], sems.at[n])
        copy.start()
        copies.append(copy)
    for copy in copies:
        copy.wait()


def fisher(place, col_levels, panel_levels, arrived, row_blocks, col_blocks, total_ex, feats):
    row_span, col_span = row_blocks * LANES, col_blocks * LANES
    sources = len(arrived)
    vmem = pl.BlockSpec(memory_space=pltpu.VMEM)
    return pl.pallas_call(
        functools.partial(fisher_kernel, sources=sources, total_ex=total_ex, feats=feats),
        in_specs=[pl.BlockSpec(memory_space=pltpu.SMEM)] + [vmem] * (2 + sources),
        out_specs=pl.BlockSpec(memory_space=pltpu.HBM),
        out_shape=jax.ShapeDtypeStruct((row_span, col_span), jnp.float32),
        scratch_shapes=[
            pltpu.VMEM((total_ex, BOTH), jnp.bfloat16),
            pltpu.VMEM((total_ex, row_span), jnp.bfloat16),
            pltpu.VMEM((total_ex, col_span), jnp.bfloat16),
            pltpu.VMEM((row_span, total_ex), jnp.bfloat16),
            pltpu.VMEM((BOTH, 2 * BOTH), jnp.float32),
            pltpu.VMEM((BOTH, 2 * BOTH), jnp.float32),
            pltpu.VMEM((2 * total_ex, col_span), jnp.bfloat16),
            pltpu.VMEM((row_span, col_span), jnp.float32),
            pltpu.SemaphoreType.DMA((col_span // BOTH,)),
        ],
        compiler_params=pltpu.CompilerParams(vmem_limit_bytes=32 * 2**20),
        name="fisher",
    )(place, col_levels, panel_levels, *arrived)


def swap(block, axis, mask):
    size = lax.axis_size(axis)
    return lax.ppermute(block, axis, [(n, n ^ mask) for n in range(size)])


def shift(block, axis, hops):
    size = lax.axis_size(axis)
    return lax.ppermute(block, axis, [(n, (n + hops) % size) for n in range(size)])


def last_first(count):
    return [*range(1, count)][-1:] + [*range(1, count)][:-1]


def shards(activations, out_grads, proj_in, proj_out, damp_level):
    local_ex = activations.shape[0]
    feats = proj_in.shape[1] * proj_out.shape[1]
    n_rows = lax.axis_size("row")
    n_cols = lax.axis_size("col")
    total_ex = local_ex * n_rows * n_cols
    row_at = lax.axis_index("row")
    col_at = lax.axis_index("col")
    blocks = feats // LANES
    row_blocks = blocks // n_rows
    col_blocks = blocks // n_cols

    levels = damp_level.astype(jnp.float32).reshape(1, feats)
    col_levels = lax.dynamic_slice_in_dim(levels, col_at * col_blocks * LANES, col_blocks * LANES, axis=1)
    place = jnp.stack([row_at, col_at]).astype(jnp.int32)

    packed = project(activations, out_grads, proj_in, proj_out)
    along = [packed] + [shift(packed, "col", hops) for hops in last_first(n_cols)]
    line = jnp.concatenate(along, axis=1)

    common = [
        lax.dynamic_slice_in_dim(line, col_at * col_blocks, col_blocks),
        line[: BOTH // LANES],
        line[blocks:],
    ]
    pairs = n_rows // 2
    pair_at = row_at // 2

    def bundle(pair):
        wanted = lax.dynamic_slice_in_dim(line, pair * 2 * row_blocks, 2 * row_blocks)
        return jnp.concatenate([wanted] + common)

    got = [bundle(pair_at)] + [swap(bundle(pair_at ^ mask), "row", 2 * mask) for mask in last_first(pairs)]
    arrived = got + [swap(piece, "row", 1) for piece in got]
    return fisher(
        place, col_levels, levels[:, :BOTH], arrived, row_blocks, col_blocks, total_ex, feats
    )


def solution(mesh):
    return jax.shard_map(
        shards,
        mesh=mesh,
        in_specs=(P(("row", "col"), None, None), P(("row", "col"), None, None), P(), P(), P()),
        out_specs=P("row", "col"),
        check_vma=False,
    )
```

```python
import functools
import itertools

import jax
import jax.numpy as jnp
from jax import lax
from jax.experimental import pallas as pl
from jax.experimental.pallas import tpu as pltpu
from jax.sharding import PartitionSpec as P

PANEL = 128
BOTH = 2 * PANEL
LANES = 128
SUB = 8
STRIP = 64
AHEAD = 1
FILL = 2

damp_coef = 0.25

HIGHEST = lax.Precision.HIGHEST
FIRSTS = (((0,), (0,)), ((), ()))
LASTS = (((1,), (1,)), ((), ()))
PLAIN = (((1,), (0,)), ((), ()))


def mxu(left, right, dims=PLAIN):
    return lax.dot_general(left, right, dims, preferred_element_type=jnp.float32)


def halves(value):
    high = value.astype(jnp.bfloat16)
    return high, (value - high.astype(jnp.float32)).astype(jnp.bfloat16)


CUTS = 8


def thirds(value):
    high = value.astype(jnp.bfloat16)
    return (high, *halves(value - high.astype(jnp.float32)))


def project_kernel(
    act_hbm, out_hbm, in_hbm, proj_hbm, packed_ref, act_buf, out_buf, in_buf, proj_buf, sems, *, local_ex, tok_len
):
    _, tokens, chunk = act_buf.shape
    rank_dim = in_buf.shape[1]
    pieces = (in_hbm, in_buf), (act_hbm, act_buf), (proj_hbm, proj_buf), (out_hbm, out_buf)
    copies = [
        [
            pltpu.make_async_copy(whole.at[:, pl.ds(n * chunk, chunk)], buf.at[n], sems.at[n, which])
            for which, (whole, buf) in enumerate(pieces)
        ]
        for n in range(CUTS)
    ]
    for group in copies:
        for copy in group:
            copy.start()
    a_proj = jnp.zeros((tokens, rank_dim), jnp.float32)
    g_proj = jnp.zeros((tokens, rank_dim), jnp.float32)
    for n, group in enumerate(copies):
        for copy in group:
            copy.wait()
        a_proj += mxu(act_buf[n], in_buf[n], LASTS)
        g_proj += mxu(out_buf[n], proj_buf[n], LASTS)
    g_turned = g_proj.T
    pairs = rank_dim * rank_dim // LANES
    example = lax.broadcasted_iota(jnp.int32, (local_ex, tokens), 0)
    owner = lax.broadcasted_iota(jnp.int32, (local_ex, tokens), 1) // tok_len
    own = jnp.where(example == owner, 1.0, 0.0).astype(jnp.float32)
    per_pair = LANES // rank_dim
    a_high, a_low = halves(a_proj)
    both = jnp.concatenate([a_high, a_low], axis=1)
    g_high, g_low = [half.astype(jnp.float32) for half in halves(g_turned * tok_len ** (-0.5))]

    def spread(source, part):
        picks = [source[n * per_pair + part : n * per_pair + part + 1, :] * own for n in range(pairs)]
        return jnp.concatenate(picks, axis=0).astype(jnp.bfloat16)

    parts = []
    for part in range(per_pair):
        wide = mxu(spread(g_high, part), both)
        parts.append(wide[:, :rank_dim] + wide[:, rank_dim:] + mxu(spread(g_low, part), a_high))
    grads = jnp.concatenate(parts, axis=1).astype(jnp.bfloat16)
    wide = grads.astype(jnp.float32)
    square = jnp.sum(wide * wide, axis=0, keepdims=True)
    rows = pairs * local_ex
    packed_ref[:rows, :] = grads
    row_at = lax.broadcasted_iota(jnp.int32, (local_ex, LANES), 0)
    first = square.astype(jnp.bfloat16).astype(jnp.float32)
    second = (square - first).astype(jnp.bfloat16).astype(jnp.float32)
    third = square - first - second
    coded = jnp.where(row_at == 0, first, jnp.where(row_at == 1, second, jnp.where(row_at == 2, third, 0.0)))
    packed_ref[rows:, :] = coded.astype(jnp.bfloat16)


def project(activations, out_grads, proj_in, proj_out):
    local_ex, tok_len, model_dim = activations.shape
    rank_dim = proj_in.shape[1]
    tokens = local_ex * tok_len
    pairs = rank_dim * rank_dim // LANES
    hbm = pl.BlockSpec(memory_space=pltpu.HBM)
    packed = pl.pallas_call(
        functools.partial(project_kernel, local_ex=local_ex, tok_len=tok_len),
        in_specs=[hbm] * 4,
        out_specs=pl.BlockSpec(memory_space=pltpu.VMEM),
        out_shape=jax.ShapeDtypeStruct(((pairs + 1) * local_ex, LANES), jnp.bfloat16),
        scratch_shapes=[
            pltpu.VMEM((CUTS, tokens, model_dim // CUTS), jnp.bfloat16),
            pltpu.VMEM((CUTS, tokens, model_dim // CUTS), jnp.bfloat16),
            pltpu.VMEM((CUTS, rank_dim, model_dim // CUTS), jnp.bfloat16),
            pltpu.VMEM((CUTS, rank_dim, model_dim // CUTS), jnp.bfloat16),
            pltpu.SemaphoreType.DMA((CUTS, 4)),
        ],
        compiler_params=pltpu.CompilerParams(vmem_limit_bytes=32 * 2**20),
        name="project",
    )(
        *[
            pltpu.with_memory_space_constraint(whole, pltpu.HBM)
            for whole in (
                activations.reshape(tokens, model_dim),
                out_grads.reshape(tokens, model_dim),
                proj_in.T,
                proj_out.T,
            )
        ]
    )
    return packed.reshape(pairs + 1, local_ex, LANES)


def eliminate(work_ref, done_ref, fillers):
    tiles = BOTH // LANES
    groups = STRIP // SUB
    sub_at = lax.broadcasted_iota(jnp.int32, (SUB, LANES), 0)
    lane_at = lax.broadcasted_iota(jnp.int32, (SUB, LANES), 1)
    for start in range(0, BOTH, STRIP):
        here = start // LANES
        live = list(range(here, tiles)) + list(range(tiles, tiles + here + 1))
        rows = [
            {t: work_ref[start + g * SUB : start + (g + 1) * SUB, t * LANES : (t + 1) * LANES] for t in live}
            for g in range(groups)
        ]
        roots = []

        def spread(block, low, high):
            lane = start % LANES + block * SUB
            return [
                {
                    g: jnp.broadcast_to(rows[g][here][:, lane + m : lane + m + 1], (SUB, LANES))
                    for g in range(low, high)
                }
                for m in range(SUB)
            ]

        cols = spread(0, 0, groups)
        for block in range(groups):
            near = min(block + 1 + (AHEAD if block < groups // 2 else 3), groups)
            ahead = spread(block + 1, block + 1, near) if block + 1 < groups else None
            pivots = jnp.ones((SUB, LANES), jnp.float32)
            inverses = []
            for j in range(SUB):
                lead = cols[j]
                pivot = lead[block][j : j + 1, :]
                inverse = 1.0 / pivot
                inverses.append(inverse)
                pivots = jnp.where(sub_at == j, pivot, pivots)
                near_scaled = lead[block] * inverse
                next_scaled = lead[block + 1] * inverse if ahead is not None else None
                for m in range(j + 1, SUB):
                    factor = near_scaled[m : m + 1, :]
                    for g in cols[m]:
                        cols[m][g] = cols[m][g] - lead[g] * factor
                if ahead is not None:
                    for m in range(SUB):
                        factor = next_scaled[m : m + 1, :]
                        for g in ahead[m]:
                            ahead[m][g] = ahead[m][g] - lead[g] * factor
                scaled = {t: rows[block][t][j : j + 1, :] * inverse for t in live}
                for g in range(block, groups):
                    weight = lead[g]
                    if g == block:
                        if j == SUB - 1:
                            continue
                        weight = jnp.where(sub_at > j, weight, 0.0)
                    for t in live:
                        rows[g][t] = rows[g][t] - weight * scaled[t]
            roots.append(lax.rsqrt(pivots))
            for filler in itertools.islice(fillers, FILL):
                filler()
            if ahead is not None:
                cols = ahead
                for m, late in enumerate(spread(block + 1, near, groups)):
                    cols[m].update(late)
        for g in range(groups):
            for t in range(2 * tiles):
                at = slice(start + g * SUB, start + (g + 1) * SUB), slice(t * LANES, (t + 1) * LANES)
                if t not in live:
                    done_ref[at] = jnp.zeros((SUB, LANES), jnp.float32)
                    continue
                value = rows[g][t] * roots[g]
                if t == here:
                    value = jnp.where(lane_at + t * LANES >= sub_at + start + g * SUB, value, 0.0)
                done_ref[at] = value
        beyond = start + STRIP
        if beyond < BOTH:
            first = beyond // LANES * LANES
            last = BOTH + -(-beyond // LANES) * LANES
            right = done_ref[start:beyond, first:last]
            rh, rm, rl = thirds(right)
            cuts = [beyond, beyond + STRIP] + ([BOTH] if beyond + STRIP < BOTH else [])
            for low, high in zip(cuts[:-1], cuts[1:]):
                left = done_ref[start:beyond, low:high]
                lh, lm, ll = thirds(left)
                work_ref[low:high, first:last] -= mxu(
                    jnp.concatenate([lh, lh, lm, lh, ll, lm], axis=0),
                    jnp.concatenate([rh, rm, rh, rl, rh, rm], axis=0),
                    FIRSTS,
                )


def fisher_kernel(
    place_ref, level_ref, panel_level_ref, *refs, sources, total_ex, feats
):
    arrived = refs[:sources]
    out_ref, g_panel, g_row, g_col, turned, work, done, weights, held, sems = refs[sources:]
    row_at, col_at = place_ref[0], place_ref[1]
    here = arrived[0].shape[1]
    row_span, col_span = held.shape
    row_blocks, col_blocks, panel_blocks = row_span // LANES, col_span // LANES, BOTH // LANES
    examples = sources * here
    col_base = 2 * row_blocks
    panel_base = col_base + col_blocks
    row_base = lax.rem(row_at, 2) * row_blocks

    def gather(target, base, blocks, n):
        for b in range(blocks):
            target[n * here : (n + 1) * here, b * LANES : (b + 1) * LANES] = arrived[n][base + b]

    total = jnp.zeros((here, LANES), jnp.float32)
    for n in range(sources):
        gather(g_panel, panel_base, panel_blocks, n)
        total += arrived[n][panel_base + panel_blocks].astype(jnp.float32)
    total_sq = jnp.sum(jnp.sum(total, axis=0, keepdims=True), axis=1, keepdims=True)
    damping = damp_coef * total_sq / (total_ex * feats)
    panel = g_panel[...]
    rows_at = lax.broadcasted_iota(jnp.int32, (BOTH, BOTH), 0)
    cols_at = lax.broadcasted_iota(jnp.int32, (BOTH, BOTH), 1)
    same = rows_at == cols_at
    work[:, :BOTH] = mxu(panel, panel, FIRSTS) * (1.0 / total_ex) + jnp.where(
        same, damping * panel_level_ref[...], 0.0
    )
    work[:, BOTH:] = jnp.where(same, 1.0, 0.0)

    def turn(first):
        turned[first : first + LANES, :] = g_row[:, first : first + LANES].T

    fillers = iter(
        [functools.partial(gather, g_row, row_base, row_blocks, n) for n in range(sources)]
        + [functools.partial(turn, first) for first in range(0, row_span, LANES)]
        + [functools.partial(gather, g_col, col_base, col_blocks, n) for n in range(sources)]
    )
    eliminate(work, done, fillers)
    for filler in fillers:
        filler()

    mixed = mxu(
        jnp.concatenate([panel, panel], axis=1), jnp.concatenate(halves(done[:, BOTH:]), axis=1), LASTS
    )
    y_high, y_low = halves(mixed)
    outer = mxu(
        jnp.concatenate([y_high, y_high, y_low], axis=1), jnp.concatenate([y_high, y_low, y_high], axis=1), LASTS
    )
    ex_rows = lax.broadcasted_iota(jnp.int32, outer.shape, 0)
    ex_cols = lax.broadcasted_iota(jnp.int32, outer.shape, 1)
    mix = (jnp.where(ex_rows == ex_cols, 1.0, 0.0) - outer * (1.0 / total_ex)) * (1.0 / total_ex)
    both = jnp.concatenate(halves(mix), axis=0)
    chunks = [slice(first, first + BOTH) for first in reversed(range(0, col_span, BOTH))]
    for lanes in chunks:
        value = mxu(both, g_col[:, lanes])
        value = value[:examples] + value[examples:]
        if lanes.start == 0:
            value = jnp.where(col_at == 0, mixed * (1.0 / total_ex), value)
        weights[:examples, lanes], weights[examples:, lanes] = halves(value)

    lower = done[:, :BOTH].T
    eye = lax.broadcasted_iota(jnp.int32, (LANES, LANES), 0) == lax.broadcasted_iota(
        jnp.int32, (LANES, LANES), 1
    )
    left = jnp.concatenate([turned[...], turned[...]], axis=1)
    copies = []
    for n, lanes in enumerate(chunks):
        value = mxu(left, weights[:, lanes])
        special = jnp.where(col_at == 0, lower, 0.0) if lanes.start == 0 else jnp.zeros_like(lower)
        held[:BOTH, lanes] = jnp.where(row_at == 0, special, value[:BOTH])
        if row_span > BOTH:
            held[BOTH:, lanes] = value[BOTH:]
        for b in range(panel_blocks):
            start = lanes.start + b * LANES
            block = col_at * col_blocks + start // LANES - row_at * row_blocks
            inside = (block >= 0) & (block < row_blocks)
            if lanes.start == 0:
                inside = inside & (col_at > 0)
            rows = pl.ds(pl.multiple_of(jnp.clip(block, 0, row_blocks - 1) * LANES, LANES), LANES)
            held[rows, start : start + LANES] += jnp.where(
                eye & inside, level_ref[:, start : start + LANES] * damping, 0.0
            )
        copy = pltpu.make_async_copy(held.at[:, lanes], out_ref.at[:, lanes], sems.at[n])
        copy.start()
        copies.append(copy)
    for copy in copies:
        copy.wait()


def fisher(place, col_levels, panel_levels, arrived, row_blocks, col_blocks, total_ex, feats):
    row_span, col_span = row_blocks * LANES, col_blocks * LANES
    sources = len(arrived)
    vmem = pl.BlockSpec(memory_space=pltpu.VMEM)
    return pl.pallas_call(
        functools.partial(fisher_kernel, sources=sources, total_ex=total_ex, feats=feats),
        in_specs=[pl.BlockSpec(memory_space=pltpu.SMEM)] + [vmem] * (2 + sources),
        out_specs=pl.BlockSpec(memory_space=pltpu.HBM),
        out_shape=jax.ShapeDtypeStruct((row_span, col_span), jnp.float32),
        scratch_shapes=[
            pltpu.VMEM((total_ex, BOTH), jnp.bfloat16),
            pltpu.VMEM((total_ex, row_span), jnp.bfloat16),
            pltpu.VMEM((total_ex, col_span), jnp.bfloat16),
            pltpu.VMEM((row_span, total_ex), jnp.bfloat16),
            pltpu.VMEM((BOTH, 2 * BOTH), jnp.float32),
            pltpu.VMEM((BOTH, 2 * BOTH), jnp.float32),
            pltpu.VMEM((2 * total_ex, col_span), jnp.bfloat16),
            pltpu.VMEM((row_span, col_span), jnp.float32),
            pltpu.SemaphoreType.DMA((col_span // BOTH,)),
        ],
        compiler_params=pltpu.CompilerParams(vmem_limit_bytes=32 * 2**20),
        name="fisher",
    )(place, col_levels, panel_levels, *arrived)


def swap(block, axis, mask):
    size = lax.axis_size(axis)
    return lax.ppermute(block, axis, [(n, n ^ mask) for n in range(size)])


def shift(block, axis, hops):
    size = lax.axis_size(axis)
    return lax.ppermute(block, axis, [(n, (n + hops) % size) for n in range(size)])


def last_first(count):
    return [*range(1, count)][-1:] + [*range(1, count)][:-1]


def shards(activations, out_grads, proj_in, proj_out, damp_level):
    local_ex = activations.shape[0]
    feats = proj_in.shape[1] * proj_out.shape[1]
    n_rows = lax.axis_size("row")
    n_cols = lax.axis_size("col")
    total_ex = local_ex * n_rows * n_cols
    row_at = lax.axis_index("row")
    col_at = lax.axis_index("col")
    blocks = feats // LANES
    row_blocks = blocks // n_rows
    col_blocks = blocks // n_cols

    levels = damp_level.astype(jnp.float32).reshape(1, feats)
    col_levels = lax.dynamic_slice_in_dim(levels, col_at * col_blocks * LANES, col_blocks * LANES, axis=1)
    place = jnp.stack([row_at, col_at]).astype(jnp.int32)

    packed = project(activations, out_grads, proj_in, proj_out)
    along = [packed] + [shift(packed, "col", hops) for hops in last_first(n_cols)]
    line = jnp.concatenate(along, axis=1)

    common = [
        lax.dynamic_slice_in_dim(line, col_at * col_blocks, col_blocks),
        line[: BOTH // LANES],
        line[blocks:],
    ]
    pairs = n_rows // 2
    pair_at = row_at // 2

    def bundle(pair):
        wanted = lax.dynamic_slice_in_dim(line, pair * 2 * row_blocks, 2 * row_blocks)
        return jnp.concatenate([wanted] + common)

    got = [bundle(pair_at)] + [swap(bundle(pair_at ^ mask), "row", 2 * mask) for mask in last_first(pairs)]
    arrived = got + [swap(piece, "row", 1) for piece in got]
    return fisher(
        place, col_levels, levels[:, :BOTH], arrived, row_blocks, col_blocks, total_ex, feats
    )


def solution(mesh):
    return jax.shard_map(
        shards,
        mesh=mesh,
        in_specs=(P(("row", "col"), None, None), P(("row", "col"), None, None), P(), P(), P()),
        out_specs=P("row", "col"),
        check_vma=False,
    )
```
